256 devices in a mesh: node: 32 (over z, x_hi, core), local: 8 (over y, x_lo).
Axes of the slice: x: 4 (x_hi: 2, x_lo: 2; x = x_hi * 2 + x_lo), y: 4, z: 8, core: 2. Of those that a mesh axis runs over, the one named last changes fastest.
Arguments:
- inputs: bfloat16 [131072, 4096], P(('node', 'local')), may hold values from -24 to 24
- cotangent: bfloat16 [131072, 1024], P(('node', 'local')), may hold values from -6 to 6
- weight: bfloat16 [4096, 1024], P(('node', 'local')), may hold values from -0.1875 to 0.1875
Outputs:
- grad_weight: float32 [2048, 2048], P(('node', 'local'))
- grad_input: bfloat16 [131072, 4096], P(('node', 'local'))
The draws below stay inside these ranges and needn't reach their ends.
All inputs are finite; a program needn't handle non-finite values.
Results may differ from the reference program's by a relative error of at most 0.03.
Values may be sent and summed in bfloat16 or wider, within the bound.
A program may use at most 128 MiB of HBM per device.

```python
import math
import jax
import jax.numpy as jnp
from jax import lax

D_WIN = 4096
KV = 1024
QBLOCK = 2048
TOK_DEV = 512
TOKENS = 131072
N_NODE = 32
N_LOCAL = 8


def spiked(drawn, stream_key, source, target, blocks, factor):
    owner, partner = [(jnp.arange(drawn.shape[dim]) // (drawn.shape[dim] // blocks)).reshape([-1 if axis == dim else 1 for axis in range(drawn.ndim)]) for dim in (source, target)]
    chosen = jax.random.permutation(stream_key, blocks)[partner]
    strong = (owner == chosen) | (owner == (partner + blocks // 2) % blocks)
    return jnp.where(strong, factor * drawn, drawn)


def level_of(own_key, shape, shards, least, largest):
    def one(position, blocks):
        heights = jax.random.uniform(jax.random.fold_in(jax.random.fold_in(own_key, 6), position), (blocks,), jnp.float32, least / len(shards), largest / len(shards))
        return jnp.repeat(jnp.exp(heights), shape[position] // blocks).reshape((-1,) + (1,) * (len(shape) - position - 1))

    level = one(*shards[0])
    for cut in shards[1:]:
        level = level * one(*cut)
    return level


def normal_values(stream_key, shape, scale, most, split=(), held_as=jnp.bfloat16):
    array = jax.random.normal(stream_key, shape, jnp.float32) * scale
    if len(split) > 0:
        array = level_of(stream_key, shape, split, -0.22, 0.18) * array
    return jnp.clip(array, min=-most, max=most).astype(held_as)


def noise_with(own_key, dims, width, most, split, heavy, kind=jnp.bfloat16):
    array = width * jax.random.normal(own_key, dims, jnp.float32)
    if split:
        array = array * level_of(own_key, dims, split, -0.22, 0.18)
    return jnp.clip(spiked(array, jax.random.fold_in(own_key, 3), *heavy), -most, most).astype(kind)


def setup_inputs(seed: int = 0) -> dict:
    seeds = jax.random.split(jax.random.key(seed), 4)
    inputs = noise_with(seeds[0], (TOKENS, D_WIN), 1.0, 24.0, ((0, 256),), (0, 1, 256, 6.0))
    cotangent = normal_values(seeds[1], (TOKENS, KV), 1.0, 6.0, ((0, 256),))
    weight = normal_values(seeds[2], (D_WIN, KV), KV ** -0.5, 0.1875, ((0, 256),))
    return {"inputs": inputs, "cotangent": cotangent, "weight": weight}


EPS_FLOOR = 1e-06
LEVELS = 127.0

def encode(values):
    scales = ((lax.optimization_barrier(jnp.max(jnp.abs(values), axis=-1)) + EPS_FLOOR) / LEVELS).astype(jnp.bfloat16)
    ratio = values / scales.astype(jnp.float32)[..., None]
    block_codes = jnp.clip(jnp.floor(ratio + 0.5), -LEVELS, LEVELS).astype(jnp.bfloat16)
    return (block_codes, scales)

def restore(block_codes, scales):
    return block_codes.astype(jnp.float32) * scales.astype(jnp.float32)[..., None]

def reference(inputs, cotangent, weight):
    blocks = D_WIN * KV // QBLOCK
    unscale = 1.0 / math.sqrt(TOKENS)

    def node_step(total, node_index):

        def local_step(first_sum, local_index):
            start = ((node_index * N_LOCAL + local_index) * TOK_DEV).astype(jnp.int32)
            rows_in = lax.dynamic_slice_in_dim(inputs, start, TOK_DEV, 0)
            rows_out = lax.dynamic_slice_in_dim(cotangent, start, TOK_DEV, 0)
            term = lax.dot_general(rows_in, rows_out, (((0,), (0,)), ((), ())), preferred_element_type=jnp.float32) * unscale
            block_codes, scales = encode(term.reshape(blocks, QBLOCK))
            return (first_sum + restore(block_codes, scales), None)
        first_sum, _ = lax.scan(local_step, jnp.zeros((blocks, QBLOCK), jnp.float32), jnp.arange(N_LOCAL, dtype=jnp.int32))
        block_codes, scales = encode(first_sum)
        return (total + restore(block_codes, scales), None)
    grad_weight, _ = lax.scan(node_step, jnp.zeros((blocks, QBLOCK), jnp.float32), jnp.arange(N_NODE, dtype=jnp.int32))

    def input_rows(group):
        start = (group * TOK_DEV).astype(jnp.int32)
        rows_out = lax.dynamic_slice_in_dim(cotangent, start, TOK_DEV, 0)
        return lax.dot_general(rows_out, weight, (((1,), (1,)), ((), ())), preferred_element_type=jnp.float32).astype(jnp.bfloat16)
    grad_input = lax.map(input_rows, jnp.arange(N_NODE * N_LOCAL, dtype=jnp.int32)).reshape(TOKENS, D_WIN)
    return (grad_weight, grad_input)
```

```python
import math

import jax
import jax.numpy as jnp
from jax import lax
from jax.experimental import pallas as pl
from jax.experimental.pallas import tpu as pltpu
from jax.sharding import PartitionSpec as P

MESH = pl.DeviceIdType.MESH
EPS_FLOOR = 1e-06
LEVELS = 127.0
BF16, F32 = jnp.bfloat16, jnp.float32

Z = 8
Y_FIRST = (3, 3, 3, 3, 2, 2, 2, 0)

EVENTS = (
    "ag1", "L0", "ag2", "L1", "ag3", "L2", "L3", "zf0",
    "YA0", "XA0", "L4", "YA1", "L5", "YA2", "XA1", "YB0", "L6", "zf1", "YA3", "XB0", "L7", "YA4", "XA2", "YB1",
    "YA5", "YB2", "C0", "XA3", "XB1", "zf2", "YA6", "YB3", "XB2", "C1", "D0", "gi0", "gi1", "gi7",
    "XA4", "XB3", "YB4", "C2", "D1", "zf3", "gi2", "gi6", "XA5", "YB5", "XB4", "C3", "D2", "XA6", "YB6", "XB5",
    "C4", "D3", "gi3", "gi5", "zf4", "XA7", "XB6", "C5", "D4", "gi4", "C6", "D5", "XB7", "D6", "E", "C7", "F",
)


def quantize(load, store, rows, unscale):
    top = jnp.abs(load(0))
    for k in range(1, 8):
        top = jnp.maximum(top, jnp.abs(load(k)))
    top = jnp.broadcast_to(jnp.max(top, axis=1, keepdims=True), (rows, 128)) * unscale
    even = lax.broadcasted_iota(jnp.int32, (rows, 128), 0) % 2 == 0
    top = jnp.maximum(top, jnp.where(even, pltpu.roll(top, rows - 1, 0), pltpu.roll(top, 1, 0)))
    scale = ((top + EPS_FLOOR) / LEVELS).astype(BF16).astype(F32)
    inverse = unscale / scale
    for k in range(8):
        code = jnp.clip(jnp.floor(load(k) * inverse + 0.5), -LEVELS, LEVELS)
        store(k, code * scale)


def kernel(unscale, inp, cot_hbm, w_hbm, gw, gi, cot, win, T, R, RB, W, F, G, CB, ZB, EB, XB, GS,
           in_sem, s_sem, r_sem, ag_s, ag_r, z_s, z_r, cx_s, cx_r, g_s, g_r, zs_s, zs_r, xb_s, xb_r, gi_sem):
    node, loc = lax.axis_index("node"), lax.axis_index("local")
    z, xh, c, y, xl = node // 4, (node // 2) % 2, node % 2, loc // 2, loc % 2

    def dev(z=z, xh=xh, c=c, y=y, xl=xl):
        return (z * 4 + xh * 2 + c, y * 2 + xl)

    def up(v, by, n):
        return (v + by + n) % n

    def to(src, dst, send, recv, target):
        return pltpu.make_async_remote_copy(
            src_ref=src, dst_ref=dst, send_sem=send, recv_sem=recv, device_id=target, device_id_type=MESH)

    def slot_z(s):
        return (z + (4 + s // 2 if s % 2 == 0 else (7 - s) // 2)) % 8

    def load_in(s, half):
        start = pl.multiple_of(slot_z(s) * 512 + half * 256, 256)
        return pltpu.make_async_copy(inp.at[:, pl.ds(start, 256)], win.at[s, half], in_sem.at[s, half])

    cot_copy = pltpu.make_async_copy(cot_hbm, cot, in_sem.at[8, 0])
    w_copy = pltpu.make_async_copy(w_hbm, W.at[z, xh, c, y, xl], in_sem.at[8, 1])
    w_copy.start()
    cot_copy.start()
    for s in range(8):
        for half in range(2):
            load_in(s, half).start()

    peers = [dev(y=up(y, 1, 4)), dev(y=up(y, -1, 4)), dev(y=up(y, 2, 4)), dev(xl=1 - xl), dev(c=1 - c),
             dev(z=up(z, 1, 8)), dev(z=up(z, -1, 8)), dev(xh=1 - xh), dev(xh=1 - xh, c=1 - c), dev(xh=1 - xh, xl=1 - xl)]
    barrier = pltpu.get_barrier_semaphore()
    for peer in peers:
        pl.semaphore_signal(barrier, inc=1, device_id=peer, device_id_type=MESH)
    pl.semaphore_wait(barrier, len(peers))

    def f32(ref):
        return ref[...].astype(F32)

    def sigma(s, q):
        return (2 * (q % 2) - 1) * (1 - 2 * (s % 2))

    def y_copy(s, q, k):
        d = sigma(s, q)
        nxt, prv, far = up(y, d, 4), up(y, -d, 4), up(y, 2, 4)
        src, dst, target = ((R.at[s, q, far], RB.at[s, q, 0:2], dev(y=nxt)),
                            (R.at[s, q, prv], RB.at[s, q, 2:4], dev(y=prv)),
                            (R.at[s, q, nxt], RB.at[s, q, 4:6], dev(y=nxt)),
                            (R.at[s, q, y, 1 - xl], RB.at[s, q, 6], dev(xl=1 - xl)))[k]
        return to(src, dst, s_sem.at[s], r_sem.at[s, q, k], target)

    def x_copy(s, q, k):
        d = sigma(s, q)
        nxt, prv, far = up(y, d, 4), up(y, -d, 4), up(y, 2, 4)
        src, dst, target = ((R.at[s, q, :, 1 - xl], RB.at[s, q, 0:4], dev(xl=1 - xl)),
                            (R.at[s, q, far, xl], RB.at[s, q, 4], dev(y=nxt)),
                            (R.at[s, q, prv, xl], RB.at[s, q, 5], dev(y=prv)),
                            (R.at[s, q, nxt, xl], RB.at[s, q, 6], dev(y=nxt)))[k]
        return to(src, dst, s_sem.at[s], r_sem.at[s, q, k], target)

    def each(lo, hi, body):
        def step(q, carry):
            body(q)
            return carry
        if hi > lo:
            lax.fori_loop(lo, hi, step, 0)

    def leaf(s):
        if s == 0:
            cot_copy.wait()
        for half in range(2):
            load_in(s, half).wait()

        def do_half(half):
            T[...] = lax.dot_general(win[s, half], cot[...], (((0,), (0,)), ((), ())), preferred_element_type=F32)

            def block(b):
                rows = pl.ds(pl.multiple_of(b * 64, 64), 64)
                q, pair = half * 2 + b // 2, (b % 2) * 2

                def store(k, value):
                    R[s, q, pl.ds(pair, 2), :, :, k * 128:(k + 1) * 128] = value.astype(BF16).reshape(2, 2, 16, 128)

                quantize(lambda k: T[rows, k * 128:(k + 1) * 128], store, 64, unscale)

            each(0, 4, block)

            def send(q2):
                q = half * 2 + q2

                @pl.when(q < Y_FIRST[s])
                def _():
                    y_copy(s, q, 0).start()
                    y_copy(s, q, 1).start()

                @pl.when(q >= Y_FIRST[s])
                def _():
                    x_copy(s, q, 0).start()

            each(0, 2, send)

        each(0, 2, do_half)

    def y_forward(s):
        def body(q):
            y_copy(s, q, 0).wait_recv()
            own = R.at[s, q, up(y, sigma(s, q), 4)]
            own[...] = (f32(own) + f32(RB.at[s, q, 0:2])).astype(BF16)
            y_copy(s, q, 2).start()
        each(0, Y_FIRST[s], body)

    def y_cross(s):
        def body(q):
            y_copy(s, q, 1).wait_recv()
            y_copy(s, q, 2).wait_recv()
            own = R.at[s, q, y, 1 - xl]
            own[...] = (f32(own) + f32(RB.at[s, q, 3 - xl]) + f32(RB.at[s, q, 5 - xl])).astype(BF16)
            y_copy(s, q, 3).start()
        each(0, Y_FIRST[s], body)

    def x_leaf(s):
        def body(q):
            x_copy(s, q, 0).wait_recv()
            for part, k in ((up(y, 2, 4), 1), (up(y, -sigma(s, q), 4), 2)):
                own = R.at[s, q, part, xl]
                own[...] = (f32(own) + f32(RB.at[s, q, part])).astype(BF16)
                x_copy(s, q, k).start()
        each(Y_FIRST[s], 4, body)

    def x_forward(s):
        def body(q):
            x_copy(s, q, 1).wait_recv()
            part = up(y, sigma(s, q), 4)
            own = R.at[s, q, part, xl]
            own[...] = (f32(own) + f32(RB.at[s, q, part]) + f32(RB.at[s, q, 4])).astype(BF16)
            x_copy(s, q, 3).start()
        each(Y_FIRST[s], 4, body)

    def g_copy(s):
        return to(G.at[s, :, 1 - c], CB.at[s], g_s.at[s], g_r.at[s], dev(c=1 - c))

    last = [(G.at[7, xh, 1 - c], dev(c=1 - c)), (G.at[7, 1 - xh, c], dev(xh=1 - xh)),
            (G.at[7, 1 - xh, 1 - c], dev(xh=1 - xh, c=1 - c)), (EB.at[1 - xh], dev(xh=1 - xh))]

    def last_copy(i):
        return to(last[i][0], XB.at[i], xb_s.at[i], xb_r.at[i], last[i][1])

    def close(s):
        def y_body(q):
            y_copy(s, q, 3).wait_recv()
            F[pl.ds(pl.multiple_of(q * 16, 16), 16), :] = (
                f32(R.at[s, q, y, xl]) + f32(RB.at[s, q, 2 + xl]) + f32(RB.at[s, q, 4 + xl]) + f32(RB.at[s, q, 6]))

        def x_body(q):
            x_copy(s, q, 2).wait_recv()
            x_copy(s, q, 3).wait_recv()
            F[pl.ds(pl.multiple_of(q * 16, 16), 16), :] = (
                f32(R.at[s, q, y, xl]) + f32(RB.at[s, q, y]) + f32(RB.at[s, q, 5]) + f32(RB.at[s, q, 6]))

        each(0, Y_FIRST[s], y_body)
        each(Y_FIRST[s], 4, x_body)

        def store(k, value):
            G[s, :, :, :, k * 128:(k + 1) * 128] = value.astype(BF16).reshape(2, 2, 16, 128)

        quantize(lambda k: F[:, k * 128:(k + 1) * 128], store, 64, 1.0)
        if s < 7:
            g_copy(s).start()
        else:
            for i in range(3):
                last_copy(i).start()

    def z_copy(s, half=0):
        right, left = dev(z=up(z, 1, 8)), dev(z=up(z, -1, 8))
        if s == 0:
            return to(G.at[0, half, c], ZB.at[0, half], zs_s.at[7 * half], zs_r.at[7 * half], left if half else right)
        return to(G.at[s, :, c], ZB.at[s], zs_s.at[s], zs_r.at[s], right if s % 2 else left)

    def pass_on(s):
        g_copy(s).wait_recv()
        if 1 <= s <= 2:
            z_copy(0, s - 1).wait_recv()
        elif s >= 3:
            z_copy(s - 2).wait_recv()
        for half in range(2):
            own = G.at[s, half, c]
            total = f32(own) + f32(CB.at[s, half])
            if s >= 3:
                total = total + f32(ZB.at[s - 2, half])
            elif s - 1 == half:
                total = total + f32(ZB.at[0, half])
            own[...] = total.astype(BF16)
        for half in range(2 if s == 0 else 1):
            z_copy(s, half).start()

    def arrive():
        z_copy(5).wait_recv()
        z_copy(6).wait_recv()
        EB[...] = (f32(ZB.at[5]) + f32(ZB.at[6])).astype(BF16)
        last_copy(3).start()

    def finish():
        for i in range(4):
            last_copy(i).wait_recv()
        total = f32(G.at[7, xh, c]) + f32(ZB.at[5, xh]) + f32(ZB.at[6, xh])
        for i in range(4):
            total = total + f32(XB.at[i])
        gw[...] = total

    def ag1(d):
        piece = W.at[z, xh, c, y, xl]
        return to(piece, piece, ag_s.at[d - 1], ag_r.at[d - 1], dev(y=up(y, d, 4)))

    def ag2():
        piece = W.at[z, xh, c, :, xl]
        return to(piece, piece, ag_s.at[3], ag_r.at[3], dev(xl=1 - xl))

    def ag3():
        piece = W.at[z, xh, c]
        return to(piece, piece, ag_s.at[4], ag_r.at[4], dev(xh=1 - xh, xl=1 - xl))

    def ring(way, k, half):
        d = 1 - 2 * way
        piece = W.at[up(z, -d * (k - 1), 8), half, c]
        i = way * 8 + (k - 1) * 2 + half
        return to(piece, piece, z_s.at[i], z_r.at[i], dev(z=up(z, d, 8)))

    def ring_steps(k):
        return [(way, k, half) for way in range(2) for half in range(2) if k < 4 or half == way]

    def swap(i):
        piece = W.at[up(z, -i, 8), :, c]
        return to(piece, piece, cx_s.at[i], cx_r.at[i], dev(c=1 - c))

    def hop(k):
        if k == 0:
            ag3().wait_recv()
            for args in ring_steps(1):
                ring(*args).start()
            swap(0).start()
            return
        for way, _, half in ring_steps(k):
            ring(way, k, half).wait_recv()
            if k < 4 and (k < 3 or half == way):
                ring(way, k + 1, half).start()
        for i in ((k, 8 - k) if k < 4 else (4,)):
            swap(i).start()

    def put(i, slot):
        start = pl.multiple_of(up(z, -i, 8) * 512, 512)
        return pltpu.make_async_copy(GS.at[slot], gi.at[:, pl.ds(start, 512)], gi_sem.at[slot])

    gi_done = []

    def grad_input(i):
        swap(i).wait_recv()
        slot = len(gi_done) % 2
        if len(gi_done) >= 2:
            put(gi_done[-2], slot).wait()
        rows = W.at[up(z, -i, 8)]

        def column(xh_):
            value = lax.dot_general(cot[...], rows[xh_].reshape(256, 1024), (((1,), (1,)), ((), ())),
                                    preferred_element_type=F32)
            GS[slot, :, pl.ds(pl.multiple_of(xh_ * 256, 256), 256)] = value.astype(BF16)

        each(0, 2, column)
        put(i, slot).start()
        gi_done.append(i)

    def start_ag():
        w_copy.wait()
        for d in (1, 3, 2):
            ag1(d).start()

    def second_ag():
        for d in (1, 3, 2):
            ag1(d).wait_recv()
        ag2().start()

    def third_ag():
        ag2().wait_recv()
        ag3().start()

    single = {"ag1": start_ag, "ag2": second_ag, "ag3": third_ag, "E": arrive, "F": finish}
    numbered = {"L": leaf, "YA": y_forward, "XA": x_leaf, "YB": y_cross, "XB": x_forward, "C": close, "D": pass_on,
                "zf": hop, "gi": grad_input}
    for event in EVENTS:
        if event in single:
            single[event]()
        else:
            numbered[event[:-1]](int(event[-1]))

    for i in gi_done[-2:]:
        put(i, gi_done.index(i) % 2).wait()
    for s in range(8):
        pltpu.make_async_copy(RB.at[s], RB.at[s], s_sem.at[s]).wait()
    for d in (1, 3, 2):
        ag1(d).wait_send()
    ag2().wait_send()
    ag3().wait_send()
    for k in range(1, 5):
        for args in ring_steps(k):
            ring(*args).wait_send()
    for i in range(8):
        swap(i).wait_send()
    for s in range(7):
        g_copy(s).wait_send()
        for half in range(2 if s == 0 else 1):
            z_copy(s, half).wait_send()
    for i in range(4):
        last_copy(i).wait_send()


def local(unscale, inputs, cotangent, weight):
    dma = pltpu.SemaphoreType.DMA
    hbm = pl.BlockSpec(memory_space=pl.ANY)
    grad_weight, grad_input = pl.pallas_call(
        lambda *refs: kernel(unscale, *refs),
        out_shape=(jax.ShapeDtypeStruct((16, 1024), F32), jax.ShapeDtypeStruct((512, 4096), BF16)),
        in_specs=[hbm] * 3,
        out_specs=(pl.BlockSpec(memory_space=pltpu.VMEM), hbm),
        scratch_shapes=[
            pltpu.VMEM((512, 1024), BF16),
            pltpu.VMEM((8, 2, 512, 256), BF16),
            pltpu.VMEM((256, 1024), F32),
            pltpu.VMEM((8, 4, 4, 2, 16, 1024), BF16),
            pltpu.VMEM((8, 4, 7, 16, 1024), BF16),
            pltpu.VMEM((8, 2, 2, 4, 2, 16, 1024), BF16),
            pltpu.VMEM((64, 1024), F32),
            pltpu.VMEM((8, 2, 2, 16, 1024), BF16),
            pltpu.VMEM((7, 2, 16, 1024), BF16),
            pltpu.VMEM((7, 2, 16, 1024), BF16),
            pltpu.VMEM((2, 16, 1024), BF16),
            pltpu.VMEM((4, 16, 1024), BF16),
            pltpu.VMEM((2, 512, 512), BF16),
            dma((9, 2)), dma((8,)), dma((8, 4, 4)),
            dma((5,)), dma((5,)), dma((16,)), dma((16,)), dma((8,)), dma((8,)),
            dma((7,)), dma((7,)), dma((8,)), dma((8,)), dma((4,)), dma((4,)), dma((2,)),
        ],
        compiler_params=pltpu.CompilerParams(collective_id=0, has_side_effects=True, vmem_limit_bytes=48 << 20),
        cost_estimate=pl.CostEstimate(flops=4 * 512 * 4096 * 1024, bytes_accessed=10 << 20, transcendentals=0),
        name="exchange",
    )(inputs, cotangent, weight)
    return grad_weight.reshape(8, 2048), grad_input


def solution(mesh):
    sharded = P(("node", "local"), None)
    tokens = 512 * mesh.shape["node"] * mesh.shape["local"]
    unscale = 1.0 / math.sqrt(tokens)
    return jax.shard_map(lambda *args: local(unscale, *args), mesh=mesh, in_specs=(sharded,) * 3,
                         out_specs=(sharded,) * 2, check_vma=False)
```

```python
import math

import jax
import jax.numpy as jnp
from jax import lax
from jax.experimental import pallas as pl
from jax.experimental.pallas import tpu as pltpu
from jax.sharding import PartitionSpec as P

MESH = pl.DeviceIdType.MESH
EPS_FLOOR = 1e-06
LEVELS = 127.0
BF16, F32 = jnp.bfloat16, jnp.float32

Z = 8
Y_FIRST = (3, 3, 2, 2, 2, 2, 2, 2)

EVENTS = (
    "La0", "Lb0", "La1", "Lb1", "ha0", "La2", "Lb2", "XA0", "YA0", "XA1", "La3", "Lb3", "hb0", "ha1", "YA1", "gi0",
    "YA2", "XA2", "XB0", "La4", "Lb4", "YB0", "XB1", "hb1", "XA3", "gi1", "YA3", "gi7", "YB1", "YB2", "ha2", "XB2",
    "XA4", "La5", "Lb5", "C0", "YA4", "C1", "hb2", "XB3", "D0", "YB3", "C2", "gi2", "XB4", "La6", "Lb6", "ha3",
    "gi6", "YA5", "XA5", "YB4", "C3", "La7", "hb3", "Lb7", "YA6", "D1", "D2", "gi3", "YB5", "XA6", "XB5", "gi5",
    "C4", "ha4", "YA7", "D3", "hb4", "YB6", "D4", "XB6", "XA7", "gi4", "C5", "YB7", "C6", "D5", "XB7", "D6", "C7",
    "E", "F",
)


def quantize(load, store, rows, unscale):
    top = jnp.abs(load(0))
    for k in range(1, 8):
        top = jnp.maximum(top, jnp.abs(load(k)))
    top = jnp.broadcast_to(jnp.max(top, axis=1, keepdims=True), (rows, 128)) * unscale
    even = lax.broadcasted_iota(jnp.int32, (rows, 128), 0) % 2 == 0
    top = jnp.maximum(top, jnp.where(even, pltpu.roll(top, rows - 1, 0), pltpu.roll(top, 1, 0)))
    scale = ((top + EPS_FLOOR) / LEVELS).astype(BF16).astype(F32)
    inverse = unscale / scale
    for k in range(8):
        code = jnp.clip(jnp.floor(load(k) * inverse + 0.5), -LEVELS, LEVELS)
        store(k, code * scale)


def kernel(unscale, inp, cot_hbm, w_hbm, gw, gi, cot, win, T, R, RB, W, F, G, CB, ZB, EB, XB, GS,
           in_sem, s_sem, r_sem, ag_s, ag_r, z_s, z_r, cx_s, cx_r, g_s, g_r, zs_s, zs_r, xb_s, xb_r, gi_sem):
    node, loc = lax.axis_index("node"), lax.axis_index("local")
    z, xh, c, y, xl = node // 4, (node // 2) % 2, node % 2, loc // 2, loc % 2

    def dev(z=z, xh=xh, c=c, y=y, xl=xl):
        return (z * 4 + xh * 2 + c, y * 2 + xl)

    def up(v, by, n):
        return (v + by + n) % n

    def to(src, dst, send, recv, target):
        return pltpu.make_async_remote_copy(
            src_ref=src, dst_ref=dst, send_sem=send, recv_sem=recv, device_id=target, device_id_type=MESH)

    def slot_z(s):
        return (z + (4 + s // 2 if s % 2 == 0 else (7 - s) // 2)) % 8

    def load_in(s, half):
        start = pl.multiple_of(slot_z(s) * 512 + half * 256, 256)
        return pltpu.make_async_copy(inp.at[:, pl.ds(start, 256)], win.at[s, half], in_sem.at[s, half])

    cot_copy = pltpu.make_async_copy(cot_hbm, cot, in_sem.at[8, 0])
    w_copy = pltpu.make_async_copy(w_hbm, W.at[z, xh, c, y, xl], in_sem.at[8, 1])
    w_copy.start()
    cot_copy.start()
    for s in range(8):
        for half in range(2):
            load_in(s, half).start()

    peers = [dev(y=up(y, 1, 4)), dev(y=up(y, -1, 4)), dev(y=up(y, 2, 4)), dev(xl=1 - xl), dev(c=1 - c),
             dev(z=up(z, 1, 8)), dev(z=up(z, -1, 8)), dev(xh=1 - xh), dev(xh=1 - xh, c=1 - c), dev(xh=1 - xh, xl=1 - xl)]
    peers += [dev(y=up(y, d, 4), xl=1 - xl) for d in (1, 2, 3)]
    barrier = pltpu.get_barrier_semaphore()
    for peer in peers:
        pl.semaphore_signal(barrier, inc=1, device_id=peer, device_id_type=MESH)

    def f32(ref):
        return ref[...].astype(F32)

    def sigma(s, q):
        return (2 * (q % 2) - 1) * (1 - 2 * (s % 2))

    def y_copy(s, q, k):
        d = sigma(s, q)
        nxt, prv, far = up(y, d, 4), up(y, -d, 4), up(y, 2, 4)
        src, dst, target = ((R.at[s, q, far], RB.at[s, q, 0:2], dev(y=nxt)),
                            (R.at[s, q, prv], RB.at[s, q, 2:4], dev(y=prv)),
                            (R.at[s, q, nxt], RB.at[s, q, 4:6], dev(y=nxt)),
                            (R.at[s, q, y, 1 - xl], RB.at[s, q, 6], dev(xl=1 - xl)))[k]
        return to(src, dst, s_sem.at[s], r_sem.at[s, q, k], target)

    def x_copy(s, q, k):
        d = sigma(s, q)
        nxt, prv, far = up(y, d, 4), up(y, -d, 4), up(y, 2, 4)
        src, dst, target = ((R.at[s, q, :, 1 - xl], RB.at[s, q, 0:4], dev(xl=1 - xl)),
                            (R.at[s, q, far, xl], RB.at[s, q, 4], dev(y=nxt)),
                            (R.at[s, q, prv, xl], RB.at[s, q, 5], dev(y=prv)),
                            (R.at[s, q, nxt, xl], RB.at[s, q, 6], dev(y=nxt)))[k]
        return to(src, dst, s_sem.at[s], r_sem.at[s, q, k], target)

    def each(lo, hi, body):
        def step(q, carry):
            body(q)
            return carry
        if hi > lo:
            lax.fori_loop(lo, hi, step, 0)

    def leaf(s, half):
        if s == 0 and half == 0:
            cot_copy.wait()
        load_in(s, half).wait()
        T[...] = lax.dot_general(win[s, half], cot[...], (((0,), (0,)), ((), ())), preferred_element_type=F32)

        def block(b):
            rows = pl.ds(pl.multiple_of(b * 64, 64), 64)
            q, pair = half * 2 + b // 2, (b % 2) * 2

            def store(k, value):
                R[s, q, pl.ds(pair, 2), :, :, k * 128:(k + 1) * 128] = value.astype(BF16).reshape(2, 2, 16, 128)

            quantize(lambda k: T[rows, k * 128:(k + 1) * 128], store, 64, unscale)

        each(0, 4, block)
        if s == 0 and half == 0:
            pl.semaphore_wait(barrier, len(peers))
            w_copy.wait()
            for i in range(7):
                ag1(i).start()
        for q in (half * 2, half * 2 + 1):
            if q < Y_FIRST[s]:
                y_copy(s, q, 0).start()
                y_copy(s, q, 1).start()
            else:
                x_copy(s, q, 0).start()

    def y_forward(s):
        def body(q):
            y_copy(s, q, 0).wait_recv()
            own = R.at[s, q, up(y, sigma(s, q), 4)]
            own[...] = (f32(own) + f32(RB.at[s, q, 0:2])).astype(BF16)
            y_copy(s, q, 2).start()
        each(0, Y_FIRST[s], body)

    def y_cross(s):
        def body(q):
            y_copy(s, q, 1).wait_recv()
            y_copy(s, q, 2).wait_recv()
            own = R.at[s, q, y, 1 - xl]
            own[...] = (f32(own) + f32(RB.at[s, q, 3 - xl]) + f32(RB.at[s, q, 5 - xl])).astype(BF16)
            y_copy(s, q, 3).start()
        each(0, Y_FIRST[s], body)

    def x_leaf(s):
        def body(q):
            x_copy(s, q, 0).wait_recv()
            for part, k in ((up(y, 2, 4), 1), (up(y, -sigma(s, q), 4), 2)):
                own = R.at[s, q, part, xl]
                own[...] = (f32(own) + f32(RB.at[s, q, part])).astype(BF16)
                x_copy(s, q, k).start()
        each(Y_FIRST[s], 4, body)

    def x_forward(s):
        def body(q):
            x_copy(s, q, 1).wait_recv()
            part = up(y, sigma(s, q), 4)
            own = R.at[s, q, part, xl]
            own[...] = (f32(own) + f32(RB.at[s, q, part]) + f32(RB.at[s, q, 4])).astype(BF16)
            x_copy(s, q, 3).start()
        each(Y_FIRST[s], 4, body)

    def g_copy(s):
        return to(G.at[s, :, 1 - c], CB.at[s], g_s.at[s], g_r.at[s], dev(c=1 - c))

    last = [(G.at[7, xh, 1 - c], dev(c=1 - c)), (G.at[7, 1 - xh, c], dev(xh=1 - xh)),
            (G.at[7, 1 - xh, 1 - c], dev(xh=1 - xh, c=1 - c)), (EB.at[1 - xh], dev(xh=1 - xh))]

    def last_copy(i):
        return to(last[i][0], XB.at[i], xb_s.at[i], xb_r.at[i], last[i][1])

    def close(s):
        def y_body(q):
            y_copy(s, q, 3).wait_recv()
            F[pl.ds(pl.multiple_of(q * 16, 16), 16), :] = (
                f32(R.at[s, q, y, xl]) + f32(RB.at[s, q, 2 + xl]) + f32(RB.at[s, q, 4 + xl]) + f32(RB.at[s, q, 6]))

        def x_body(q):
            x_copy(s, q, 2).wait_recv()
            x_copy(s, q, 3).wait_recv()
            F[pl.ds(pl.multiple_of(q * 16, 16), 16), :] = (
                f32(R.at[s, q, y, xl]) + f32(RB.at[s, q, y]) + f32(RB.at[s, q, 5]) + f32(RB.at[s, q, 6]))

        each(0, Y_FIRST[s], y_body)
        each(Y_FIRST[s], 4, x_body)

        def store(k, value):
            G[s, :, :, :, k * 128:(k + 1) * 128] = value.astype(BF16).reshape(2, 2, 16, 128)

        quantize(lambda k: F[:, k * 128:(k + 1) * 128], store, 64, 1.0)
        if s < 7:
            g_copy(s).start()
        else:
            for i in range(3):
                last_copy(i).start()

    def z_copy(s, half=0):
        right, left = dev(z=up(z, 1, 8)), dev(z=up(z, -1, 8))
        if s == 0:
            return to(G.at[0, half, c], ZB.at[0, half], zs_s.at[7 * half], zs_r.at[7 * half], left if half else right)
        return to(G.at[s, :, c], ZB.at[s], zs_s.at[s], zs_r.at[s], right if s % 2 else left)

    def pass_on(s):
        g_copy(s).wait_recv()
        if 1 <= s <= 2:
            z_copy(0, s - 1).wait_recv()
        elif s >= 3:
            z_copy(s - 2).wait_recv()
        for half in range(2):
            own = G.at[s, half, c]
            total = f32(own) + f32(CB.at[s, half])
            if s >= 3:
                total = total + f32(ZB.at[s - 2, half])
            elif s - 1 == half:
                total = total + f32(ZB.at[0, half])
            own[...] = total.astype(BF16)
        for half in range(2 if s == 0 else 1):
            z_copy(s, half).start()

    def arrive():
        z_copy(5).wait_recv()
        z_copy(6).wait_recv()
        EB[...] = (f32(ZB.at[5]) + f32(ZB.at[6])).astype(BF16)
        last_copy(3).start()

    def finish():
        for i in range(4):
            last_copy(i).wait_recv()
        total = f32(G.at[7, xh, c]) + f32(ZB.at[5, xh]) + f32(ZB.at[6, xh])
        for i in range(4):
            total = total + f32(XB.at[i])
        gw[...] = total

    def ag1(i):
        piece = W.at[z, xh, c, y, xl]
        dy, dx = (i + 1) // 2, (i + 1) % 2
        return to(piece, piece, ag_s.at[i], ag_r.at[i], dev(y=up(y, dy, 4), xl=(xl + dx) % 2))

    def ag3():
        piece = W.at[z, xh, c]
        return to(piece, piece, ag_s.at[7], ag_r.at[7], dev(xh=1 - xh, xl=1 - xl))

    def ring(way, k, half):
        d = 1 - 2 * way
        piece = W.at[up(z, -d * (k - 1), 8), half, c]
        i = way * 8 + (k - 1) * 2 + half
        return to(piece, piece, z_s.at[i], z_r.at[i], dev(z=up(z, d, 8)))

    def swap(i, half):
        piece = W.at[up(z, -i, 8), half, c]
        return to(piece, piece, cx_s.at[i * 2 + half], cx_r.at[i * 2 + half], dev(c=1 - c))

    def hop(k, half):
        if k == 0:
            for way in range(2):
                ring(way, 1, half).start()
            swap(0, half).start()
        elif k < 4:
            for way in range(2):
                ring(way, k, half).wait_recv()
                if k < 3:
                    ring(way, k + 1, half).start()
            if k == 3:
                ring(half, 4, half).start()
            swap(k, half).start()
            swap(8 - k, half).start()
        else:
            ring(half, 4, half).wait_recv()
            swap(4, half).start()

    def own_hop(k):
        if k == 0:
            for i in range(7):
                ag1(i).wait_recv()
            ag3().start()
        hop(k, xh)

    def other_hop(k):
        if k == 0:
            ag3().wait_recv()
        hop(k, 1 - xh)

    def put(i, slot):
        start = pl.multiple_of(up(z, -i, 8) * 512, 512)
        return pltpu.make_async_copy(GS.at[slot], gi.at[:, pl.ds(start, 512)], gi_sem.at[slot])

    gi_done = []

    def grad_input(i):
        swap(i, 0).wait_recv()
        swap(i, 1).wait_recv()
        slot = len(gi_done) % 2
        if len(gi_done) >= 2:
            put(gi_done[-2], slot).wait()
        rows = W.at[up(z, -i, 8)]

        def column(xh_):
            value = lax.dot_general(cot[...], rows[xh_].reshape(256, 1024), (((1,), (1,)), ((), ())),
                                    preferred_element_type=F32)
            GS[slot, :, pl.ds(pl.multiple_of(xh_ * 256, 256), 256)] = value.astype(BF16)

        each(0, 2, column)
        put(i, slot).start()
        gi_done.append(i)

    single = {"E": arrive, "F": finish}
    numbered = {"La": lambda s: leaf(s, 0), "Lb": lambda s: leaf(s, 1), "YA": y_forward, "XA": x_leaf, "YB": y_cross,
                "XB": x_forward, "C": close, "D": pass_on, "ha": own_hop, "hb": other_hop, "gi": grad_input}
    for event in EVENTS:
        if event in single:
            single[event]()
        else:
            numbered[event[:-1]](int(event[-1]))

    for i in gi_done[-2:]:
        put(i, gi_done.index(i) % 2).wait()
    for s in range(8):
        pltpu.make_async_copy(RB.at[s], RB.at[s], s_sem.at[s]).wait()
    for i in range(7):
        ag1(i).wait_send()
    ag3().wait_send()
    for half in range(2):
        for way in range(2):
            for k in range(1, 5 if way == half else 4):
                ring(way, k, half).wait_send()
        for i in range(8):
            swap(i, half).wait_send()
    for s in range(7):
        g_copy(s).wait_send()
        for half in range(2 if s == 0 else 1):
            z_copy(s, half).wait_send()
    for i in range(4):
        last_copy(i).wait_send()


def deliver(sums, products, grad_weight, grad_input, sem):
    copies = [pltpu.make_async_copy(products.at[pl.ds(i * 64, 64)], grad_input.at[pl.ds(i * 64, 64)], sem.at[i])
              for i in range(8)]
    for copy in copies:
        copy.start()
    for row in range(16):
        start = row % 2 * 1024
        grad_weight[row // 2:row // 2 + 1, start:start + 1024] = sums[row:row + 1, :]
    for copy in copies:
        copy.wait()


def local(unscale, inputs, cotangent, weight):
    dma = pltpu.SemaphoreType.DMA
    hbm = pl.BlockSpec(memory_space=pltpu.HBM)
    anywhere = pl.BlockSpec(memory_space=pl.ANY)
    vmem = pl.BlockSpec(memory_space=pltpu.VMEM)
    sums, products = pl.pallas_call(
        lambda *refs: kernel(unscale, *refs),
        out_shape=(jax.ShapeDtypeStruct((16, 1024), F32), jax.ShapeDtypeStruct((512, 4096), BF16)),
        in_specs=[hbm] * 3,
        out_specs=(vmem, anywhere),
        scratch_shapes=[
            pltpu.VMEM((512, 1024), BF16),
            pltpu.VMEM((8, 2, 512, 256), BF16),
            pltpu.VMEM((256, 1024), F32),
            pltpu.VMEM((8, 4, 4, 2, 16, 1024), BF16),
            pltpu.VMEM((8, 4, 7, 16, 1024), BF16),
            pltpu.VMEM((8, 2, 2, 4, 2, 16, 1024), BF16),
            pltpu.VMEM((64, 1024), F32),
            pltpu.VMEM((8, 2, 2, 16, 1024), BF16),
            pltpu.VMEM((7, 2, 16, 1024), BF16),
            pltpu.VMEM((7, 2, 16, 1024), BF16),
            pltpu.VMEM((2, 16, 1024), BF16),
            pltpu.VMEM((4, 16, 1024), BF16),
            pltpu.VMEM((2, 512, 512), BF16),
            dma((9, 2)), dma((8,)), dma((8, 4, 4)),
            dma((8,)), dma((8,)), dma((16,)), dma((16,)), dma((16,)), dma((16,)),
            dma((7,)), dma((7,)), dma((8,)), dma((8,)), dma((4,)), dma((4,)), dma((2,)),
        ],
        compiler_params=pltpu.CompilerParams(collective_id=0, has_side_effects=True, vmem_limit_bytes=48 << 20),
        cost_estimate=pl.CostEstimate(flops=4 * 512 * 4096 * 1024, bytes_accessed=10 << 20, transcendentals=0),
        name="exchange",
    )(inputs, cotangent, weight)
    return pl.pallas_call(
        deliver,
        out_shape=(jax.ShapeDtypeStruct((8, 2048), F32), jax.ShapeDtypeStruct((512, 4096), BF16)),
        in_specs=[vmem, vmem],
        out_specs=(vmem, hbm),
        scratch_shapes=[dma((8,))],
        compiler_params=pltpu.CompilerParams(vmem_limit_bytes=16 << 20),
        name="deliver",
    )(sums, products)


def solution(mesh):
    sharded = P(("node", "local"), None)
    tokens = 512 * mesh.shape["node"] * mesh.shape["local"]
    unscale = 1.0 / math.sqrt(tokens)
    return jax.shard_map(lambda *args: local(unscale, *args), mesh=mesh, in_specs=(sharded,) * 3,
                         out_specs=(sharded,) * 2, check_vma=False)
```

```python
import math

import jax
import jax.numpy as jnp
from jax import lax
from jax.experimental import pallas as pl
from jax.experimental.pallas import tpu as pltpu
from jax.sharding import PartitionSpec as P

MESH = pl.DeviceIdType.MESH
EPS_FLOOR = 1e-06
LEVELS = 127.0
BF16, F32 = jnp.bfloat16, jnp.float32

Z = 8
FAR = 3
Y_FIRST = (3, 2, 2, 2, 2, 2, 2, 2)

EVENTS = (
    "AG", "Lb0", "La3", "Lb2", "A2", "La0", "Lb1", "La2", "Lb3", "La1", "ha0", "YA0", "La4", "ha1", "Lb4", "YA1",
    "hb0", "XA1", "XA0", "YB0", "Lb6", "XA3", "XA2", "YA3", "XB0", "YA2", "XB1", "La6", "XA4", "ha2", "La5", "YB1",
    "La7", "Lb5", "YB2", "hb1", "XB2", "YA6", "gi0", "C0", "C1", "ha3", "YA4", "XB3", "Lb7", "YA5", "YB3", "hb2",
    "D0", "XA5", "gi1", "XA6", "XB4", "YB4", "C2", "YA7", "gi6", "ha4", "YB6", "D2", "D1", "YB5", "XA7", "gi7",
    "XB5", "C3", "XB6", "C4", "hb3", "YB7", "D3", "XB7", "D4", "gi2", "C5", "C6", "C7", "D5", "hb4", "D6", "gi5",
    "gi3", "gi4", "F",
)


def quantize(load, store, rows, unscale):
    top = jnp.abs(load(0))
    for k in range(1, 8):
        top = jnp.maximum(top, jnp.abs(load(k)))
    top = jnp.broadcast_to(jnp.max(top, axis=1, keepdims=True), (rows, 128)) * unscale
    even = lax.broadcasted_iota(jnp.int32, (rows, 128), 0) % 2 == 0
    top = jnp.maximum(top, jnp.where(even, pltpu.roll(top, rows - 1, 0), pltpu.roll(top, 1, 0)))
    scale = ((top + EPS_FLOOR) / LEVELS).astype(BF16).astype(F32)
    inverse = unscale / scale
    for k in range(8):
        code = jnp.clip(jnp.floor(load(k) * inverse + 0.5), -LEVELS, LEVELS)
        store(k, code * scale)


def kernel(unscale, inp, cot_hbm, w_hbm, gw, gi, cot, win, T, R, RB, W, F, G, CB, ZB, XB, GS,
           in_sem, s_sem, r_sem, ag_s, ag_r, ac_s, ac_r, z_s, z_r, cx_s, cx_r, g_s, g_r, zs_s, zs_r, xb_s, xb_r, gi_sem):
    node, loc = lax.axis_index("node"), lax.axis_index("local")
    z, xh, c, y, xl = node // 4, (node // 2) % 2, node % 2, loc // 2, loc % 2

    def dev(z=z, xh=xh, c=c, y=y, xl=xl):
        return (z * 4 + xh * 2 + c, y * 2 + xl)

    def up(v, by, n):
        return (v + by + n) % n

    def to(src, dst, send, recv, target):
        return pltpu.make_async_remote_copy(
            src_ref=src, dst_ref=dst, send_sem=send, recv_sem=recv, device_id=target, device_id_type=MESH)

    def slot_z(s):
        return (z + (4 + s // 2 if s % 2 == 0 else (7 - s) // 2)) % 8

    def load_in(s, half):
        start = pl.multiple_of(slot_z(s) * 512 + half * 256, 256)
        return pltpu.make_async_copy(inp.at[:, pl.ds(start, 256)], win.at[s, half], in_sem.at[s, half])

    cot_copy = pltpu.make_async_copy(cot_hbm, cot, in_sem.at[8, 0])
    w_copy = pltpu.make_async_copy(w_hbm, W.at[z, xh, c, y, xl], in_sem.at[8, 1])
    w_copy.start()
    cot_copy.start()
    for event in EVENTS:
        if event[:2] in ("La", "Lb"):
            load_in(int(event[2]), "ab".index(event[1])).start()

    peers = [dev(y=up(y, 1, 4)), dev(y=up(y, -1, 4)), dev(y=up(y, 2, 4)), dev(xl=1 - xl), dev(c=1 - c),
             dev(z=up(z, 1, 8)), dev(z=up(z, -1, 8)), dev(xh=1 - xh), dev(xh=1 - xh, c=1 - c), dev(xh=1 - xh, xl=1 - xl)]
    peers += [dev(z=up(z, d, 8), xh=1 - xh) for d in (1, -1)]
    barrier = pltpu.get_barrier_semaphore()
    for peer in peers:
        pl.semaphore_signal(barrier, inc=1, device_id=peer, device_id_type=MESH)

    def f32(ref):
        return ref[...].astype(F32)

    def sigma(s, q):
        return (2 * (q % 2) - 1) * (1 - 2 * (s % 2))

    def y_copy(s, q, k):
        d = sigma(s, q)
        nxt, prv, far = up(y, d, 4), up(y, -d, 4), up(y, 2, 4)
        src, dst, target = ((R.at[s, q, far], RB.at[s, q, 0:2], dev(y=nxt)),
                            (R.at[s, q, prv], RB.at[s, q, 2:4], dev(y=prv)),
                            (R.at[s, q, nxt], RB.at[s, q, 4:6], dev(y=nxt)),
                            (R.at[s, q, y, 1 - xl], RB.at[s, q, 6], dev(xl=1 - xl)))[k]
        return to(src, dst, s_sem.at[s], r_sem.at[s, q, k], target)

    def x_copy(s, q, k):
        d = sigma(s, q)
        nxt, prv, far = up(y, d, 4), up(y, -d, 4), up(y, 2, 4)
        src, dst, target = ((R.at[s, q, :, 1 - xl], RB.at[s, q, 0:4], dev(xl=1 - xl)),
                            (R.at[s, q, far, xl], RB.at[s, q, 4], dev(y=nxt)),
                            (R.at[s, q, prv, xl], RB.at[s, q, 5], dev(y=prv)),
                            (R.at[s, q, nxt, xl], RB.at[s, q, 6], dev(y=nxt)))[k]
        return to(src, dst, s_sem.at[s], r_sem.at[s, q, k], target)

    def each(lo, hi, body):
        def step(q, carry):
            body(q)
            return carry
        if hi > lo:
            lax.fori_loop(lo, hi, step, 0)

    def leaf(s, half):
        load_in(s, half).wait()
        T[...] = lax.dot_general(win[s, half], cot[...], (((0,), (0,)), ((), ())), preferred_element_type=F32)

        def block(b):
            rows = pl.ds(pl.multiple_of(b * 64, 64), 64)
            q, pair = half * 2 + b // 2, (b % 2) * 2

            def store(k, value):
                R[s, q, pl.ds(pair, 2), :, :, k * 128:(k + 1) * 128] = value.astype(BF16).reshape(2, 2, 16, 128)

            quantize(lambda k: T[rows, k * 128:(k + 1) * 128], store, 64, unscale)

        each(0, 4, block)
        for q in (half * 2, half * 2 + 1):
            if q < Y_FIRST[s]:
                y_copy(s, q, 0).start()
                y_copy(s, q, 1).start()
            else:
                x_copy(s, q, 0).start()

    def y_forward(s):
        def body(q):
            y_copy(s, q, 0).wait_recv()
            own = R.at[s, q, up(y, sigma(s, q), 4)]
            own[...] = (f32(own) + f32(RB.at[s, q, 0:2])).astype(BF16)
            y_copy(s, q, 2).start()
        each(0, Y_FIRST[s], body)

    def y_cross(s):
        def body(q):
            y_copy(s, q, 1).wait_recv()
            y_copy(s, q, 2).wait_recv()
            own = R.at[s, q, y, 1 - xl]
            own[...] = (f32(own) + f32(RB.at[s, q, 3 - xl]) + f32(RB.at[s, q, 5 - xl])).astype(BF16)
            y_copy(s, q, 3).start()
        each(0, Y_FIRST[s], body)

    def x_leaf(s):
        def body(q):
            x_copy(s, q, 0).wait_recv()
            for part, k in ((up(y, 2, 4), 1), (up(y, -sigma(s, q), 4), 2)):
                own = R.at[s, q, part, xl]
                own[...] = (f32(own) + f32(RB.at[s, q, part])).astype(BF16)
                x_copy(s, q, k).start()
        each(Y_FIRST[s], 4, body)

    def x_forward(s):
        def body(q):
            x_copy(s, q, 1).wait_recv()
            part = up(y, sigma(s, q), 4)
            own = R.at[s, q, part, xl]
            own[...] = (f32(own) + f32(RB.at[s, q, part]) + f32(RB.at[s, q, 4])).astype(BF16)
            x_copy(s, q, 3).start()
        each(Y_FIRST[s], 4, body)

    def g_copy(s):
        return to(G.at[s, :, 1 - c], CB.at[s], g_s.at[s], g_r.at[s], dev(c=1 - c))

    last = [(G.at[7, xh, 1 - c], dev(c=1 - c)), (G.at[7, 1 - xh, c], dev(xh=1 - xh)),
            (G.at[7, 1 - xh, 1 - c], dev(xh=1 - xh, c=1 - c))]

    def last_copy(i):
        return to(last[i][0], XB.at[i], xb_s.at[i], xb_r.at[i], last[i][1])

    def close(s):
        def y_body(q):
            y_copy(s, q, 3).wait_recv()
            F[pl.ds(pl.multiple_of(q * 16, 16), 16), :] = (
                f32(R.at[s, q, y, xl]) + f32(RB.at[s, q, 2 + xl]) + f32(RB.at[s, q, 4 + xl]) + f32(RB.at[s, q, 6]))

        def x_body(q):
            x_copy(s, q, 2).wait_recv()
            x_copy(s, q, 3).wait_recv()
            F[pl.ds(pl.multiple_of(q * 16, 16), 16), :] = (
                f32(R.at[s, q, y, xl]) + f32(RB.at[s, q, y]) + f32(RB.at[s, q, 5]) + f32(RB.at[s, q, 6]))

        each(0, Y_FIRST[s], y_body)
        each(Y_FIRST[s], 4, x_body)

        def store(k, value):
            G[s, :, :, :, k * 128:(k + 1) * 128] = value.astype(BF16).reshape(2, 2, 16, 128)

        quantize(lambda k: F[:, k * 128:(k + 1) * 128], store, 64, 1.0)
        if s < 7:
            g_copy(s).start()
        else:
            for i in (2, 1, 0):
                last_copy(i).start()

    def z_copy(s, part=0):
        i = s + 7 * part
        target = up(z, 1, 8) if s % 2 or (s == 0 and part == 0) else up(z, -1, 8)
        if s == 0:
            return to(G.at[0, part, c], ZB.at[0, part], zs_s.at[i], zs_r.at[i], dev(z=target))
        if s < 5:
            return to(G.at[s, :, c], ZB.at[s], zs_s.at[i], zs_r.at[i], dev(z=target))
        half = (1 - xh) if part else xh
        return to(G.at[s, half, c], ZB.at[s, part], zs_s.at[i], zs_r.at[i], dev(z=target, xh=half))

    def z_parts(s):
        return (0,) if 1 <= s < 5 else (1, 0)

    def pass_on(s):
        g_copy(s).wait_recv()
        if 1 <= s <= 2:
            z_copy(0, s - 1).wait_recv()
        elif s >= 3:
            z_copy(s - 2).wait_recv()
        for half in range(2):
            own = G.at[s, half, c]
            total = f32(own) + f32(CB.at[s, half])
            if s >= 3:
                total = total + f32(ZB.at[s - 2, half])
            elif s - 1 == half:
                total = total + f32(ZB.at[0, half])
            own[...] = total.astype(BF16)
        for part in z_parts(s):
            z_copy(s, part).start()

    def finish():
        total = f32(G.at[7, xh, c])
        for s in (5, 6):
            for part in (0, 1):
                z_copy(s, part).wait_recv()
                total = total + f32(ZB.at[s, part])
        for i in range(3):
            last_copy(i).wait_recv()
            total = total + f32(XB.at[i])
        gw[...] = total

    def ag1(i, whose=0):
        piece = W.at[z, xh, c, y, (xl + whose) % 2]
        sems = ag_s.at[whose * 4 + i], ag_r.at[whose * 4 + i]
        return to(piece, piece, *sems, dev(y=up(y, i, 4), xl=(xl + (i == 0)) % 2))

    def ring(way, k, half):
        d = 1 - 2 * way
        piece = W.at[up(z, -d * (k - 1), 8), half, c]
        i = way * 8 + (k - 1) * 2 + half
        return to(piece, piece, z_s.at[i], z_r.at[i], dev(z=up(z, d, 8)))

    def swap(i, half):
        piece = W.at[up(z, -i, 8), half, c]
        return to(piece, piece, cx_s.at[i * 2 + half], cx_r.at[i * 2 + half], dev(c=1 - c))

    def across(i):
        piece = W.at[up(z, -i, 8), xh, c]
        return to(piece, piece, ac_s.at[i], ac_r.at[i], dev(xh=1 - xh, xl=1 - xl))

    def from_across(i):
        piece = W.at[up(z, -i, 8), 1 - xh, c]
        to(piece, piece, ac_s.at[i], ac_r.at[i], dev(xh=1 - xh, xl=1 - xl)).wait_recv()

    def spots(k):
        return (k, 8 - k) if 0 < k < 4 else (k,)

    def own_hop(k):
        if k == 0:
            for whose in range(2):
                for i in (1, 3, 2):
                    ag1(i, whose).wait_recv()
            for way in range(2):
                ring(way, 1, xh).start()
        elif k < 4:
            for way in range(2):
                ring(way, k, xh).wait_recv()
                if k < 3:
                    ring(way, k + 1, xh).start()
            if k == 3:
                ring(c, 4, xh).start()
        else:
            ring(c, 4, xh).wait_recv()
        for i in spots(k):
            if k == 0 or k >= FAR:
                across(i).start()
            swap(i, xh).start()

    def other_hop(k):
        if k == 0 or k >= FAR:
            for i in spots(k):
                from_across(i)
        else:
            for way in range(2):
                ring(way, k, 1 - xh).wait_recv()
        if k + 1 < FAR:
            for way in range(2):
                ring(way, k + 1, 1 - xh).start()
        for i in spots(k):
            swap(i, 1 - xh).start()

    def put(i, slot):
        start = pl.multiple_of(up(z, -i, 8) * 512, 512)
        return pltpu.make_async_copy(GS.at[slot], gi.at[:, pl.ds(start, 512)], gi_sem.at[slot])

    gi_done = []

    def grad_input(i):
        swap(i, 0).wait_recv()
        swap(i, 1).wait_recv()
        slot = len(gi_done) % 2
        if len(gi_done) >= 2:
            put(gi_done[-2], slot).wait()
        rows = W.at[up(z, -i, 8)]

        def column(xh_):
            value = lax.dot_general(cot[...], rows[xh_].reshape(256, 1024), (((1,), (1,)), ((), ())),
                                    preferred_element_type=F32)
            GS[slot, :, pl.ds(pl.multiple_of(xh_ * 256, 256), 256)] = value.astype(BF16)

        each(0, 2, column)
        put(i, slot).start()
        gi_done.append(i)

    def open_up():
        pl.semaphore_wait(barrier, len(peers))
        w_copy.wait()
        for i in (0, 2, 1, 3):
            ag1(i).start()
        cot_copy.wait()

    def second_ag():
        ag1(0).wait_recv()
        for i in (2, 1, 3):
            ag1(i, 1).start()

    single = {"AG": open_up, "A2": second_ag, "F": finish}
    numbered = {"La": lambda s: leaf(s, 0), "Lb": lambda s: leaf(s, 1), "YA": y_forward, "XA": x_leaf, "YB": y_cross,
                "XB": x_forward, "C": close, "D": pass_on, "ha": own_hop, "hb": other_hop, "gi": grad_input}
    for event in EVENTS:
        if event in single:
            single[event]()
        else:
            numbered[event[:-1]](int(event[-1]))

    for i in gi_done[-2:]:
        put(i, gi_done.index(i) % 2).wait()
    for s in range(8):
        pltpu.make_async_copy(RB.at[s], RB.at[s], s_sem.at[s]).wait()
    for whose in range(2):
        for i in range(whose, 4):
            ag1(i, whose).wait_send()
    for i in range(8):
        for half in range(2):
            swap(i, half).wait_send()
    for i in (0,) + tuple(range(FAR, 9 - FAR)):
        across(i).wait_send()
    for k in range(1, 4):
        for way in range(2):
            ring(way, k, xh).wait_send()
            if k < FAR:
                ring(way, k, 1 - xh).wait_send()
    ring(c, 4, xh).wait_send()
    for s in range(7):
        g_copy(s).wait_send()
        for part in z_parts(s):
            z_copy(s, part).wait_send()
    for i in range(3):
        last_copy(i).wait_send()


def deliver(sums, products, grad_weight, grad_input, sem):
    copies = [pltpu.make_async_copy(products.at[pl.ds(i * 64, 64)], grad_input.at[pl.ds(i * 64, 64)], sem.at[i])
              for i in range(8)]
    for copy in copies:
        copy.start()
    for row in range(16):
        start = row % 2 * 1024
        grad_weight[row // 2:row // 2 + 1, start:start + 1024] = sums[row:row + 1, :]
    for copy in copies:
        copy.wait()


def local(unscale, inputs, cotangent, weight):
    dma = pltpu.SemaphoreType.DMA
    hbm = pl.BlockSpec(memory_space=pltpu.HBM)
    anywhere = pl.BlockSpec(memory_space=pl.ANY)
    vmem = pl.BlockSpec(memory_space=pltpu.VMEM)
    sums, products = pl.pallas_call(
        lambda *refs: kernel(unscale, *refs),
        out_shape=(jax.ShapeDtypeStruct((16, 1024), F32), jax.ShapeDtypeStruct((512, 4096), BF16)),
        in_specs=[hbm] * 3,
        out_specs=(vmem, anywhere),
        scratch_shapes=[
            pltpu.VMEM((512, 1024), BF16),
            pltpu.VMEM((8, 2, 512, 256), BF16),
            pltpu.VMEM((256, 1024), F32),
            pltpu.VMEM((8, 4, 4, 2, 16, 1024), BF16),
            pltpu.VMEM((8, 4, 7, 16, 1024), BF16),
            pltpu.VMEM((8, 2, 2, 4, 2, 16, 1024), BF16),
            pltpu.VMEM((64, 1024), F32),
            pltpu.VMEM((8, 2, 2, 16, 1024), BF16),
            pltpu.VMEM((7, 2, 16, 1024), BF16),
            pltpu.VMEM((7, 2, 16, 1024), BF16),
            pltpu.VMEM((3, 16, 1024), BF16),
            pltpu.VMEM((2, 512, 512), BF16),
            dma((9, 2)), dma((8,)), dma((8, 4, 4)),
            dma((8,)), dma((8,)), dma((8,)), dma((8,)), dma((16,)), dma((16,)), dma((16,)), dma((16,)),
            dma((7,)), dma((7,)), dma((14,)), dma((14,)), dma((3,)), dma((3,)), dma((2,)),
        ],
        compiler_params=pltpu.CompilerParams(collective_id=0, has_side_effects=True, vmem_limit_bytes=48 << 20),
        cost_estimate=pl.CostEstimate(flops=4 * 512 * 4096 * 1024, bytes_accessed=10 << 20, transcendentals=0),
        name="exchange",
    )(*[pltpu.with_memory_space_constraint(array, pltpu.HBM) for array in (inputs, cotangent, weight)])
    return pl.pallas_call(
        deliver,
        out_shape=(jax.ShapeDtypeStruct((8, 2048), F32), jax.ShapeDtypeStruct((512, 4096), BF16)),
        in_specs=[vmem, vmem],
        out_specs=(vmem, hbm),
        scratch_shapes=[dma((8,))],
        compiler_params=pltpu.CompilerParams(vmem_limit_bytes=16 << 20),
        name="deliver",
    )(sums, products)


def solution(mesh):
    sharded = P(("node", "local"), None)
    tokens = 512 * mesh.shape["node"] * mesh.shape["local"]
    unscale = 1.0 / math.sqrt(tokens)
    return jax.shard_map(lambda *args: local(unscale, *args), mesh=mesh, in_specs=(sharded,) * 3,
                         out_specs=(sharded,) * 2, check_vma=False)
```

```python
import math

import jax
import jax.numpy as jnp
from jax import lax
from jax.experimental import pallas as pl
from jax.experimental.pallas import tpu as pltpu
from jax.sharding import PartitionSpec as P

MESH = pl.DeviceIdType.MESH
EPS_FLOOR = 1e-06
LEVELS = 127.0
BF16, F32 = jnp.bfloat16, jnp.float32

Z = 8
FAR = 3
Y_FIRST = (3, 2, 2, 2, 2, 2, 2, 2)

EVENTS = (
    "AG", "Lb0", "La3", "Lb2", "A2", "La0", "Lb1", "La2", "Lb3", "La1", "ha0", "YA0", "La4", "ha1", "Lb4", "YA1",
    "hb0", "XA1", "XA0", "YB0", "Lb6", "XA3", "XA2", "YA3", "XB0", "YA2", "XB1", "La6", "XA4", "ha2", "La5", "YB1",
    "La7", "Lb5", "YB2", "hb1", "XB2", "YA6", "gi0", "C0", "C1", "ha3", "YA4", "XB3", "Lb7", "YA5", "YB3", "hb2",
    "D0", "XA5", "gi1", "XA6", "XB4", "YB4", "C2", "YA7", "gi6", "ha4", "YB6", "D2", "D1", "YB5", "XA7", "gi7",
    "XB5", "C3", "XB6", "C4", "hb3", "YB7", "D3", "XB7", "D4", "gi2", "C5", "C6", "C7", "D5", "hb4", "D6", "gi5",
    "gi3", "gi4", "F",
)


def quantize(load, store, rows, unscale):
    top = jnp.abs(load(0))
    for k in range(1, 8):
        top = jnp.maximum(top, jnp.abs(load(k)))
    top = jnp.broadcast_to(jnp.max(top, axis=1, keepdims=True), (rows, 128)) * unscale
    even = lax.broadcasted_iota(jnp.int32, (rows, 128), 0) % 2 == 0
    top = jnp.maximum(top, jnp.where(even, pltpu.roll(top, rows - 1, 0), pltpu.roll(top, 1, 0)))
    scale = ((top + EPS_FLOOR) / LEVELS).astype(BF16).astype(F32)
    inverse = unscale / scale
    for k in range(8):
        code = jnp.clip(jnp.floor(load(k) * inverse + 0.5), -LEVELS, LEVELS)
        store(k, code * scale)


def kernel(unscale, inp, cot_hbm, w_hbm, gw, gi, cot, win, T, R, RB, W, F, G, CB, ZB, XB, GS,
           in_sem, s_sem, r_sem, ag_s, ag_r, ac_s, ac_r, z_s, z_r, cx_s, cx_r, g_s, g_r, zs_s, zs_r, xb_s, xb_r, gi_sem):
    node, loc = lax.axis_index("node"), lax.axis_index("local")
    z, xh, c, y, xl = node // 4, (node // 2) % 2, node % 2, loc // 2, loc % 2

    def dev(z=z, xh=xh, c=c, y=y, xl=xl):
        return (z * 4 + xh * 2 + c, y * 2 + xl)

    def up(v, by, n):
        return (v + by + n) % n

    def to(src, dst, send, recv, target):
        return pltpu.make_async_remote_copy(
            src_ref=src, dst_ref=dst, send_sem=send, recv_sem=recv, device_id=target, device_id_type=MESH)

    def slot_z(s):
        return (z + (4 + s // 2 if s % 2 == 0 else (7 - s) // 2)) % 8

    def load_in(s, half):
        start = pl.multiple_of(slot_z(s) * 512 + half * 256, 256)
        return pltpu.make_async_copy(inp.at[:, pl.ds(start, 256)], win.at[s, half], in_sem.at[s, half])

    peers = [dev(y=up(y, 1, 4)), dev(y=up(y, -1, 4)), dev(y=up(y, 2, 4)), dev(xl=1 - xl), dev(c=1 - c),
             dev(z=up(z, 1, 8)), dev(z=up(z, -1, 8)), dev(xh=1 - xh), dev(xh=1 - xh, c=1 - c), dev(xh=1 - xh, xl=1 - xl)]
    peers += [dev(z=up(z, d, 8), xh=1 - xh) for d in (1, -1)]
    barrier = pltpu.get_barrier_semaphore()
    for peer in peers:
        pl.semaphore_signal(barrier, inc=1, device_id=peer, device_id_type=MESH)

    cot_copies = [pltpu.make_async_copy(cot_hbm.at[pl.ds(i * 128, 128)], cot.at[pl.ds(i * 128, 128)], in_sem.at[9 + i // 2, i % 2])
                  for i in range(4)]
    w_copy = pltpu.make_async_copy(w_hbm, W.at[z, xh, c, y, xl], in_sem.at[8, 1])
    w_copy.start()
    leaves = [load_in(int(event[2]), "ab".index(event[1])) for event in EVENTS if event[:2] in ("La", "Lb")]
    for copy in cot_copies + leaves[:2]:
        copy.start()

    def f32(ref):
        return ref[...].astype(F32)

    def sigma(s, q):
        return (2 * (q % 2) - 1) * (1 - 2 * (s % 2))

    def y_copy(s, q, k):
        d = sigma(s, q)
        nxt, prv, far = up(y, d, 4), up(y, -d, 4), up(y, 2, 4)
        src, dst, target = ((R.at[s, q, far], RB.at[s, q, 0:2], dev(y=nxt)),
                            (R.at[s, q, prv], RB.at[s, q, 2:4], dev(y=prv)),
                            (R.at[s, q, nxt], RB.at[s, q, 4:6], dev(y=nxt)),
                            (R.at[s, q, y, 1 - xl], RB.at[s, q, 6], dev(xl=1 - xl)))[k]
        return to(src, dst, s_sem.at[s], r_sem.at[s, q, k], target)

    def x_copy(s, q, k):
        d = sigma(s, q)
        nxt, prv, far = up(y, d, 4), up(y, -d, 4), up(y, 2, 4)
        src, dst, target = ((R.at[s, q, :, 1 - xl], RB.at[s, q, 0:4], dev(xl=1 - xl)),
                            (R.at[s, q, far, xl], RB.at[s, q, 4], dev(y=nxt)),
                            (R.at[s, q, prv, xl], RB.at[s, q, 5], dev(y=prv)),
                            (R.at[s, q, nxt, xl], RB.at[s, q, 6], dev(y=nxt)))[k]
        return to(src, dst, s_sem.at[s], r_sem.at[s, q, k], target)

    def each(lo, hi, body):
        def step(q, carry):
            body(q)
            return carry
        if hi > lo:
            lax.fori_loop(lo, hi, step, 0)

    def leaf(s, half):
        load_in(s, half).wait()
        T[...] = lax.dot_general(win[s, half], cot[...], (((0,), (0,)), ((), ())), preferred_element_type=F32)

        def block(b):
            rows = pl.ds(pl.multiple_of(b * 64, 64), 64)
            q, pair = half * 2 + b // 2, (b % 2) * 2

            def store(k, value):
                R[s, q, pl.ds(pair, 2), :, :, k * 128:(k + 1) * 128] = value.astype(BF16).reshape(2, 2, 16, 128)

            quantize(lambda k: T[rows, k * 128:(k + 1) * 128], store, 64, unscale)

        each(0, 4, block)
        for q in (half * 2, half * 2 + 1):
            if q < Y_FIRST[s]:
                y_copy(s, q, 0).start()
                y_copy(s, q, 1).start()
            else:
                x_copy(s, q, 0).start()

    def y_forward(s):
        def body(q):
            y_copy(s, q, 0).wait_recv()
            own = R.at[s, q, up(y, sigma(s, q), 4)]
            own[...] = (f32(own) + f32(RB.at[s, q, 0:2])).astype(BF16)
            y_copy(s, q, 2).start()
        each(0, Y_FIRST[s], body)

    def y_cross(s):
        def body(q):
            y_copy(s, q, 1).wait_recv()
            y_copy(s, q, 2).wait_recv()
            own = R.at[s, q, y, 1 - xl]
            own[...] = (f32(own) + f32(RB.at[s, q, 3 - xl]) + f32(RB.at[s, q, 5 - xl])).astype(BF16)
            y_copy(s, q, 3).start()
        each(0, Y_FIRST[s], body)

    def x_leaf(s):
        def body(q):
            x_copy(s, q, 0).wait_recv()
            for part, k in ((up(y, 2, 4), 1), (up(y, -sigma(s, q), 4), 2)):
                own = R.at[s, q, part, xl]
                own[...] = (f32(own) + f32(RB.at[s, q, part])).astype(BF16)
                x_copy(s, q, k).start()
        each(Y_FIRST[s], 4, body)

    def x_forward(s):
        def body(q):
            x_copy(s, q, 1).wait_recv()
            part = up(y, sigma(s, q), 4)
            own = R.at[s, q, part, xl]
            own[...] = (f32(own) + f32(RB.at[s, q, part]) + f32(RB.at[s, q, 4])).astype(BF16)
            x_copy(s, q, 3).start()
        each(Y_FIRST[s], 4, body)

    def g_copy(s):
        return to(G.at[s, :, 1 - c], CB.at[s], g_s.at[s], g_r.at[s], dev(c=1 - c))

    last = [(G.at[7, xh, 1 - c], dev(c=1 - c)), (G.at[7, 1 - xh, c], dev(xh=1 - xh)),
            (G.at[7, 1 - xh, 1 - c], dev(xh=1 - xh, c=1 - c))]

    def last_copy(i):
        return to(last[i][0], XB.at[i], xb_s.at[i], xb_r.at[i], last[i][1])

    def close(s):
        def y_body(q):
            y_copy(s, q, 3).wait_recv()
            F[pl.ds(pl.multiple_of(q * 16, 16), 16), :] = (
                f32(R.at[s, q, y, xl]) + f32(RB.at[s, q, 2 + xl]) + f32(RB.at[s, q, 4 + xl]) + f32(RB.at[s, q, 6]))

        def x_body(q):
            x_copy(s, q, 2).wait_recv()
            x_copy(s, q, 3).wait_recv()
            F[pl.ds(pl.multiple_of(q * 16, 16), 16), :] = (
                f32(R.at[s, q, y, xl]) + f32(RB.at[s, q, y]) + f32(RB.at[s, q, 5]) + f32(RB.at[s, q, 6]))

        each(0, Y_FIRST[s], y_body)
        each(Y_FIRST[s], 4, x_body)

        def store(k, value):
            G[s, :, :, :, k * 128:(k + 1) * 128] = value.astype(BF16).reshape(2, 2, 16, 128)

        quantize(lambda k: F[:, k * 128:(k + 1) * 128], store, 64, 1.0)
        if s < 7:
            g_copy(s).start()
        else:
            for i in (2, 1, 0):
                last_copy(i).start()

    def z_copy(s, part=0):
        i = s + 7 * part
        target = up(z, 1, 8) if s % 2 or (s == 0 and part == 0) else up(z, -1, 8)
        if s == 0:
            return to(G.at[0, part, c], ZB.at[0, part], zs_s.at[i], zs_r.at[i], dev(z=target))
        if s < 5:
            return to(G.at[s, :, c], ZB.at[s], zs_s.at[i], zs_r.at[i], dev(z=target))
        half = (1 - xh) if part else xh
        return to(G.at[s, half, c], ZB.at[s, part], zs_s.at[i], zs_r.at[i], dev(z=target, xh=half))

    def z_parts(s):
        return (0,) if 1 <= s < 5 else (1, 0)

    def pass_on(s):
        g_copy(s).wait_recv()
        if 1 <= s <= 2:
            z_copy(0, s - 1).wait_recv()
        elif s >= 3:
            z_copy(s - 2).wait_recv()
        for half in range(2):
            own = G.at[s, half, c]
            total = f32(own) + f32(CB.at[s, half])
            if s >= 3:
                total = total + f32(ZB.at[s - 2, half])
            elif s - 1 == half:
                total = total + f32(ZB.at[0, half])
            own[...] = total.astype(BF16)
        for part in z_parts(s):
            z_copy(s, part).start()

    def finish():
        total = f32(G.at[7, xh, c])
        for s in (5, 6):
            for part in (0, 1):
                z_copy(s, part).wait_recv()
                total = total + f32(ZB.at[s, part])
        for i in range(3):
            last_copy(i).wait_recv()
            total = total + f32(XB.at[i])
        gw[...] = total

    def ag1(i, whose=0):
        piece = W.at[z, xh, c, y, (xl + whose) % 2]
        sems = ag_s.at[whose * 4 + i], ag_r.at[whose * 4 + i]
        return to(piece, piece, *sems, dev(y=up(y, i, 4), xl=(xl + (i == 0)) % 2))

    def ring(way, k, half):
        d = 1 - 2 * way
        piece = W.at[up(z, -d * (k - 1), 8), half, c]
        i = way * 8 + (k - 1) * 2 + half
        return to(piece, piece, z_s.at[i], z_r.at[i], dev(z=up(z, d, 8)))

    def swap(i, half):
        piece = W.at[up(z, -i, 8), half, c]
        return to(piece, piece, cx_s.at[i * 2 + half], cx_r.at[i * 2 + half], dev(c=1 - c))

    def across(i):
        piece = W.at[up(z, -i, 8), xh, c]
        return to(piece, piece, ac_s.at[i], ac_r.at[i], dev(xh=1 - xh, xl=1 - xl))

    def from_across(i):
        piece = W.at[up(z, -i, 8), 1 - xh, c]
        to(piece, piece, ac_s.at[i], ac_r.at[i], dev(xh=1 - xh, xl=1 - xl)).wait_recv()

    def spots(k):
        return (k, 8 - k) if 0 < k < 4 else (k,)

    def own_hop(k):
        if k == 0:
            for whose in range(2):
                for i in (1, 3, 2):
                    ag1(i, whose).wait_recv()
            for way in range(2):
                ring(way, 1, xh).start()
        elif k < 4:
            for way in range(2):
                ring(way, k, xh).wait_recv()
                if k < 3:
                    ring(way, k + 1, xh).start()
            if k == 3:
                ring(c, 4, xh).start()
        else:
            ring(c, 4, xh).wait_recv()
        for i in spots(k):
            if k == 0 or k >= FAR:
                across(i).start()
            swap(i, xh).start()

    def other_hop(k):
        if k == 0 or k >= FAR:
            for i in spots(k):
                from_across(i)
        else:
            for way in range(2):
                ring(way, k, 1 - xh).wait_recv()
        if k + 1 < FAR:
            for way in range(2):
                ring(way, k + 1, 1 - xh).start()
        for i in spots(k):
            swap(i, 1 - xh).start()

    def put(i, slot):
        start = pl.multiple_of(up(z, -i, 8) * 512, 512)
        return pltpu.make_async_copy(GS.at[slot], gi.at[:, pl.ds(start, 512)], gi_sem.at[slot])

    gi_done = []

    def grad_input(i):
        swap(i, 0).wait_recv()
        swap(i, 1).wait_recv()
        slot = len(gi_done) % 2
        if len(gi_done) >= 2:
            put(gi_done[-2], slot).wait()
        rows = W.at[up(z, -i, 8)]

        def column(xh_):
            value = lax.dot_general(cot[...], rows[xh_].reshape(256, 1024), (((1,), (1,)), ((), ())),
                                    preferred_element_type=F32)
            GS[slot, :, pl.ds(pl.multiple_of(xh_ * 256, 256), 256)] = value.astype(BF16)

        each(0, 2, column)
        put(i, slot).start()
        gi_done.append(i)

    def open_up():
        pl.semaphore_wait(barrier, len(peers))
        w_copy.wait()
        for i in (0, 2, 1, 3):
            ag1(i).start()
        for copy in leaves[2:]:
            copy.start()
        for copy in cot_copies:
            copy.wait()

    def second_ag():
        ag1(0).wait_recv()
        for i in (2, 1, 3):
            ag1(i, 1).start()

    single = {"AG": open_up, "A2": second_ag, "F": finish}
    numbered = {"La": lambda s: leaf(s, 0), "Lb": lambda s: leaf(s, 1), "YA": y_forward, "XA": x_leaf, "YB": y_cross,
                "XB": x_forward, "C": close, "D": pass_on, "ha": own_hop, "hb": other_hop, "gi": grad_input}
    for event in EVENTS:
        if event in single:
            single[event]()
        else:
            numbered[event[:-1]](int(event[-1]))

    for i in gi_done[-2:]:
        put(i, gi_done.index(i) % 2).wait()
    for s in range(8):
        pltpu.make_async_copy(RB.at[s], RB.at[s], s_sem.at[s]).wait()
    for whose in range(2):
        for i in range(whose, 4):
            ag1(i, whose).wait_send()
    for i in range(8):
        for half in range(2):
            swap(i, half).wait_send()
    for i in (0,) + tuple(range(FAR, 9 - FAR)):
        across(i).wait_send()
    for k in range(1, 4):
        for way in range(2):
            ring(way, k, xh).wait_send()
            if k < FAR:
                ring(way, k, 1 - xh).wait_send()
    ring(c, 4, xh).wait_send()
    for s in range(7):
        g_copy(s).wait_send()
        for part in z_parts(s):
            z_copy(s, part).wait_send()
    for i in range(3):
        last_copy(i).wait_send()


def deliver(sums, products, grad_weight, grad_input, sem):
    copies = [pltpu.make_async_copy(products.at[pl.ds(i * 64, 64)], grad_input.at[pl.ds(i * 64, 64)], sem.at[i])
              for i in range(8)]
    for copy in copies:
        copy.start()
    for row in range(16):
        start = row % 2 * 1024
        grad_weight[row // 2:row // 2 + 1, start:start + 1024] = sums[row:row + 1, :]
    for copy in copies:
        copy.wait()


def local(unscale, inputs, cotangent, weight):
    dma = pltpu.SemaphoreType.DMA
    hbm = pl.BlockSpec(memory_space=pltpu.HBM)
    anywhere = pl.BlockSpec(memory_space=pl.ANY)
    vmem = pl.BlockSpec(memory_space=pltpu.VMEM)
    sums, products = pl.pallas_call(
        lambda *refs: kernel(unscale, *refs),
        out_shape=(jax.ShapeDtypeStruct((16, 1024), F32), jax.ShapeDtypeStruct((512, 4096), BF16)),
        in_specs=[hbm] * 3,
        out_specs=(vmem, anywhere),
        scratch_shapes=[
            pltpu.VMEM((512, 1024), BF16),
            pltpu.VMEM((8, 2, 512, 256), BF16),
            pltpu.VMEM((256, 1024), F32),
            pltpu.VMEM((8, 4, 4, 2, 16, 1024), BF16),
            pltpu.VMEM((8, 4, 7, 16, 1024), BF16),
            pltpu.VMEM((8, 2, 2, 4, 2, 16, 1024), BF16),
            pltpu.VMEM((64, 1024), F32),
            pltpu.VMEM((8, 2, 2, 16, 1024), BF16),
            pltpu.VMEM((7, 2, 16, 1024), BF16),
            pltpu.VMEM((7, 2, 16, 1024), BF16),
            pltpu.VMEM((3, 16, 1024), BF16),
            pltpu.VMEM((2, 512, 512), BF16),
            dma((11, 2)), dma((8,)), dma((8, 4, 4)),
            dma((8,)), dma((8,)), dma((8,)), dma((8,)), dma((16,)), dma((16,)), dma((16,)), dma((16,)),
            dma((7,)), dma((7,)), dma((14,)), dma((14,)), dma((3,)), dma((3,)), dma((2,)),
        ],
        compiler_params=pltpu.CompilerParams(collective_id=0, has_side_effects=True, vmem_limit_bytes=48 << 20),
        cost_estimate=pl.CostEstimate(flops=4 * 512 * 4096 * 1024, bytes_accessed=10 << 20, transcendentals=0),
        name="exchange",
    )(*[pltpu.with_memory_space_constraint(array, pltpu.HBM) for array in (inputs, cotangent, weight)])
    return pl.pallas_call(
        deliver,
        out_shape=(jax.ShapeDtypeStruct((8, 2048), F32), jax.ShapeDtypeStruct((512, 4096), BF16)),
        in_specs=[vmem, vmem],
        out_specs=(vmem, hbm),
        scratch_shapes=[dma((8,))],
        compiler_params=pltpu.CompilerParams(vmem_limit_bytes=16 << 20),
        name="deliver",
    )(sums, products)


def solution(mesh):
    sharded = P(("node", "local"), None)
    tokens = 512 * mesh.shape["node"] * mesh.shape["local"]
    unscale = 1.0 / math.sqrt(tokens)
    return jax.shard_map(lambda *args: local(unscale, *args), mesh=mesh, in_specs=(sharded,) * 3,
                         out_specs=(sharded,) * 2, check_vma=False)
```

```python
import math

import jax
import jax.numpy as jnp
from jax import lax
from jax.experimental import pallas as pl
from jax.experimental.pallas import tpu as pltpu
from jax.sharding import PartitionSpec as P

MESH = pl.DeviceIdType.MESH
EPS_FLOOR = 1e-06
LEVELS = 127.0
BF16, F32 = jnp.bfloat16, jnp.float32

Z = 8
FAR = 2
Y_FIRST = (3, 2, 2, 2, 2, 2, 2, 2)

EVENTS = (
    "AG", "Lb0", "La3", "Lb2", "A2", "La0", "Lb1", "La2", "Lb3", "La1", "ha0", "YA0", "La4", "ha1", "Lb4", "YA1",
    "hb0", "XA1", "XA0", "YB0", "Lb6", "XA3", "XA2", "YA3", "XB0", "YA2", "XB1", "La6", "XA4", "ha2", "La5", "YB1",
    "La7", "Lb5", "YB2", "hb1", "XB2", "YA6", "gi0", "C0", "C1", "ha3", "YA4", "XB3", "Lb7", "YA5", "YB3", "hb2",
    "D0", "XA5", "gi1", "XA6", "XB4", "YB4", "C2", "YA7", "gi6", "ha4", "YB6", "D2", "D1", "YB5", "XA7", "gi7",
    "XB5", "C3", "XB6", "C4", "hb3", "YB7", "D3", "XB7", "D4", "gi2", "C5", "C6", "C7", "D5", "hb4", "D6", "gi5",
    "gi3", "gi4", "F",
)


def quantize(load, store, rows, unscale):
    top = jnp.abs(load(0))
    for k in range(1, 8):
        top = jnp.maximum(top, jnp.abs(load(k)))
    top = jnp.broadcast_to(jnp.max(top, axis=1, keepdims=True), (rows, 128)) * unscale
    even = lax.broadcasted_iota(jnp.int32, (rows, 128), 0) % 2 == 0
    top = jnp.maximum(top, jnp.where(even, pltpu.roll(top, rows - 1, 0), pltpu.roll(top, 1, 0)))
    scale = ((top + EPS_FLOOR) / LEVELS).astype(BF16).astype(F32)
    inverse = unscale / scale
    for k in range(8):
        code = jnp.clip(jnp.floor(load(k) * inverse + 0.5), -LEVELS, LEVELS)
        store(k, code * scale)


def kernel(unscale, inp, cot_hbm, w_hbm, gw, gi, cot, win, T, R, RB, W, F, G, CB, ZB, XB, GS,
           in_sem, s_sem, r_sem, ag_s, ag_r, ac_s, ac_r, z_s, z_r, cx_s, cx_r, g_s, g_r, zs_s, zs_r, xb_s, xb_r, gi_sem):
    node, loc = lax.axis_index("node"), lax.axis_index("local")
    z, xh, c, y, xl = node // 4, (node // 2) % 2, node % 2, loc // 2, loc % 2

    def dev(z=z, xh=xh, c=c, y=y, xl=xl):
        return (z * 4 + xh * 2 + c, y * 2 + xl)

    def up(v, by, n):
        return (v + by + n) % n

    def to(src, dst, send, recv, target):
        return pltpu.make_async_remote_copy(
            src_ref=src, dst_ref=dst, send_sem=send, recv_sem=recv, device_id=target, device_id_type=MESH)

    def slot_z(s):
        return (z + (4 + s // 2 if s % 2 == 0 else (7 - s) // 2)) % 8

    def load_in(s, half):
        start = pl.multiple_of(slot_z(s) * 512 + half * 256, 256)
        return pltpu.make_async_copy(inp.at[:, pl.ds(start, 256)], win.at[s, half], in_sem.at[s, half])

    peers = [dev(y=up(y, 1, 4)), dev(y=up(y, -1, 4)), dev(y=up(y, 2, 4)), dev(xl=1 - xl), dev(c=1 - c),
             dev(z=up(z, 1, 8)), dev(z=up(z, -1, 8)), dev(xh=1 - xh), dev(xh=1 - xh, c=1 - c), dev(xh=1 - xh, xl=1 - xl)]
    peers += [dev(z=up(z, d, 8), xh=1 - xh) for d in (1, -1)]
    barrier = pltpu.get_barrier_semaphore()
    for peer in peers:
        pl.semaphore_signal(barrier, inc=1, device_id=peer, device_id_type=MESH)

    cot_copies = [pltpu.make_async_copy(cot_hbm.at[pl.ds(i * 128, 128)], cot.at[pl.ds(i * 128, 128)], in_sem.at[9 + i // 2, i % 2])
                  for i in range(4)]
    w_copy = pltpu.make_async_copy(w_hbm, W.at[z, xh, c, y, xl], in_sem.at[8, 1])
    w_copy.start()
    leaves = [load_in(int(event[2]), "ab".index(event[1])) for event in EVENTS if event[:2] in ("La", "Lb")]
    for copy in cot_copies + leaves[:2]:
        copy.start()

    def f32(ref):
        return ref[...].astype(F32)

    def sigma(s, q):
        return (2 * (q % 2) - 1) * (1 - 2 * (s % 2))

    def y_copy(s, q, k):
        d = sigma(s, q)
        nxt, prv, far = up(y, d, 4), up(y, -d, 4), up(y, 2, 4)
        src, dst, target = ((R.at[s, q, far], RB.at[s, q, 0:2], dev(y=nxt)),
                            (R.at[s, q, prv], RB.at[s, q, 2:4], dev(y=prv)),
                            (R.at[s, q, nxt], RB.at[s, q, 4:6], dev(y=nxt)),
                            (R.at[s, q, y, 1 - xl], RB.at[s, q, 6], dev(xl=1 - xl)))[k]
        return to(src, dst, s_sem.at[s], r_sem.at[s, q, k], target)

    def x_copy(s, q, k):
        d = sigma(s, q)
        nxt, prv, far = up(y, d, 4), up(y, -d, 4), up(y, 2, 4)
        src, dst, target = ((R.at[s, q, :, 1 - xl], RB.at[s, q, 0:4], dev(xl=1 - xl)),
                            (R.at[s, q, far, xl], RB.at[s, q, 4], dev(y=nxt)),
                            (R.at[s, q, prv, xl], RB.at[s, q, 5], dev(y=prv)),
                            (R.at[s, q, nxt, xl], RB.at[s, q, 6], dev(y=nxt)))[k]
        return to(src, dst, s_sem.at[s], r_sem.at[s, q, k], target)

    def each(lo, hi, body):
        def step(q, carry):
            body(q)
            return carry
        if hi > lo:
            lax.fori_loop(lo, hi, step, 0)

    def leaf(s, half):
        load_in(s, half).wait()
        T[...] = lax.dot_general(win[s, half], cot[...], (((0,), (0,)), ((), ())), preferred_element_type=F32)

        def block(b):
            rows = pl.ds(pl.multiple_of(b * 64, 64), 64)
            q, pair = half * 2 + b // 2, (b % 2) * 2

            def store(k, value):
                R[s, q, pl.ds(pair, 2), :, :, k * 128:(k + 1) * 128] = value.astype(BF16).reshape(2, 2, 16, 128)

            quantize(lambda k: T[rows, k * 128:(k + 1) * 128], store, 64, unscale)

        each(0, 4, block)
        for q in (half * 2, half * 2 + 1):
            if q < Y_FIRST[s]:
                y_copy(s, q, 0).start()
                y_copy(s, q, 1).start()
            else:
                x_copy(s, q, 0).start()

    def y_forward(s):
        def body(q):
            y_copy(s, q, 0).wait_recv()
            own = R.at[s, q, up(y, sigma(s, q), 4)]
            own[...] = (f32(own) + f32(RB.at[s, q, 0:2])).astype(BF16)
            y_copy(s, q, 2).start()
        each(0, Y_FIRST[s], body)

    def y_cross(s):
        def body(q):
            y_copy(s, q, 1).wait_recv()
            y_copy(s, q, 2).wait_recv()
            own = R.at[s, q, y, 1 - xl]
            own[...] = (f32(own) + f32(RB.at[s, q, 3 - xl]) + f32(RB.at[s, q, 5 - xl])).astype(BF16)
            y_copy(s, q, 3).start()
        each(0, Y_FIRST[s], body)

    def x_leaf(s):
        def body(q):
            x_copy(s, q, 0).wait_recv()
            for part, k in ((up(y, 2, 4), 1), (up(y, -sigma(s, q), 4), 2)):
                own = R.at[s, q, part, xl]
                own[...] = (f32(own) + f32(RB.at[s, q, part])).astype(BF16)
                x_copy(s, q, k).start()
        each(Y_FIRST[s], 4, body)

    def x_forward(s):
        def body(q):
            x_copy(s, q, 1).wait_recv()
            part = up(y, sigma(s, q), 4)
            own = R.at[s, q, part, xl]
            own[...] = (f32(own) + f32(RB.at[s, q, part]) + f32(RB.at[s, q, 4])).astype(BF16)
            x_copy(s, q, 3).start()
        each(Y_FIRST[s], 4, body)

    def g_copy(s):
        return to(G.at[s, :, 1 - c], CB.at[s], g_s.at[s], g_r.at[s], dev(c=1 - c))

    last = [(G.at[7, xh, 1 - c], dev(c=1 - c)), (G.at[7, 1 - xh, c], dev(xh=1 - xh)),
            (G.at[7, 1 - xh, 1 - c], dev(xh=1 - xh, c=1 - c))]

    def last_copy(i):
        return to(last[i][0], XB.at[i], xb_s.at[i], xb_r.at[i], last[i][1])

    def close(s):
        def y_body(q):
            y_copy(s, q, 3).wait_recv()
            F[pl.ds(pl.multiple_of(q * 16, 16), 16), :] = (
                f32(R.at[s, q, y, xl]) + f32(RB.at[s, q, 2 + xl]) + f32(RB.at[s, q, 4 + xl]) + f32(RB.at[s, q, 6]))

        def x_body(q):
            x_copy(s, q, 2).wait_recv()
            x_copy(s, q, 3).wait_recv()
            F[pl.ds(pl.multiple_of(q * 16, 16), 16), :] = (
                f32(R.at[s, q, y, xl]) + f32(RB.at[s, q, y]) + f32(RB.at[s, q, 5]) + f32(RB.at[s, q, 6]))

        each(0, Y_FIRST[s], y_body)
        each(Y_FIRST[s], 4, x_body)

        def store(k, value):
            G[s, :, :, :, k * 128:(k + 1) * 128] = value.astype(BF16).reshape(2, 2, 16, 128)

        quantize(lambda k: F[:, k * 128:(k + 1) * 128], store, 64, 1.0)
        if s < 7:
            g_copy(s).start()
        else:
            for i in (2, 1, 0):
                last_copy(i).start()

    def z_copy(s, part=0):
        i = s + 7 * part
        target = up(z, 1, 8) if s % 2 or (s == 0 and part == 0) else up(z, -1, 8)
        if s == 0:
            return to(G.at[0, part, c], ZB.at[0, part], zs_s.at[i], zs_r.at[i], dev(z=target))
        if s < 5:
            return to(G.at[s, :, c], ZB.at[s], zs_s.at[i], zs_r.at[i], dev(z=target))
        half = (1 - xh) if part else xh
        return to(G.at[s, half, c], ZB.at[s, part], zs_s.at[i], zs_r.at[i], dev(z=target, xh=half))

    def z_parts(s):
        return (0,) if 1 <= s < 5 else (1, 0)

    def pass_on(s):
        g_copy(s).wait_recv()
        if 1 <= s <= 2:
            z_copy(0, s - 1).wait_recv()
        elif s >= 3:
            z_copy(s - 2).wait_recv()
        for half in range(2):
            own = G.at[s, half, c]
            total = f32(own) + f32(CB.at[s, half])
            if s >= 3:
                total = total + f32(ZB.at[s - 2, half])
            elif s - 1 == half:
                total = total + f32(ZB.at[0, half])
            own[...] = total.astype(BF16)
        for part in z_parts(s):
            z_copy(s, part).start()

    def finish():
        total = f32(G.at[7, xh, c])
        for s in (5, 6):
            for part in (0, 1):
                z_copy(s, part).wait_recv()
                total = total + f32(ZB.at[s, part])
        for i in range(3):
            last_copy(i).wait_recv()
            total = total + f32(XB.at[i])
        gw[...] = total

    def ag1(i, whose=0):
        piece = W.at[z, xh, c, y, (xl + whose) % 2]
        sems = ag_s.at[whose * 4 + i], ag_r.at[whose * 4 + i]
        return to(piece, piece, *sems, dev(y=up(y, i, 4), xl=(xl + (i == 0)) % 2))

    def ring(way, k, half):
        d = 1 - 2 * way
        piece = W.at[up(z, -d * (k - 1), 8), half, c]
        i = way * 8 + (k - 1) * 2 + half
        return to(piece, piece, z_s.at[i], z_r.at[i], dev(z=up(z, d, 8)))

    def swap(i, half):
        piece = W.at[up(z, -i, 8), half, c]
        return to(piece, piece, cx_s.at[i * 2 + half], cx_r.at[i * 2 + half], dev(c=1 - c))

    def across(i):
        piece = W.at[up(z, -i, 8), xh, c]
        return to(piece, piece, ac_s.at[i], ac_r.at[i], dev(xh=1 - xh, xl=1 - xl))

    def from_across(i):
        piece = W.at[up(z, -i, 8), 1 - xh, c]
        to(piece, piece, ac_s.at[i], ac_r.at[i], dev(xh=1 - xh, xl=1 - xl)).wait_recv()

    def spots(k):
        return (k, 8 - k) if 0 < k < 4 else (k,)

    def own_hop(k):
        if k == 0:
            for whose in range(2):
                for i in (1, 3, 2):
                    ag1(i, whose).wait_recv()
            for way in range(2):
                ring(way, 1, xh).start()
        elif k < 4:
            for way in range(2):
                ring(way, k, xh).wait_recv()
                if k < 3:
                    ring(way, k + 1, xh).start()
            if k == 3:
                ring(c, 4, xh).start()
        else:
            ring(c, 4, xh).wait_recv()
        for i in spots(k):
            if k == 0 or k >= FAR:
                across(i).start()
            swap(i, xh).start()

    def other_hop(k):
        if k == 0 or k >= FAR:
            for i in spots(k):
                from_across(i)
        else:
            for way in range(2):
                ring(way, k, 1 - xh).wait_recv()
        if k + 1 < FAR:
            for way in range(2):
                ring(way, k + 1, 1 - xh).start()
        for i in spots(k):
            swap(i, 1 - xh).start()

    def put(i, slot):
        start = pl.multiple_of(up(z, -i, 8) * 512, 512)
        return pltpu.make_async_copy(GS.at[slot], gi.at[:, pl.ds(start, 512)], gi_sem.at[slot])

    gi_done = []

    def grad_input(i):
        swap(i, 0).wait_recv()
        swap(i, 1).wait_recv()
        slot = len(gi_done) % 2
        if len(gi_done) >= 2:
            put(gi_done[-2], slot).wait()
        rows = W.at[up(z, -i, 8)]

        def column(xh_):
            value = lax.dot_general(cot[...], rows[xh_].reshape(256, 1024), (((1,), (1,)), ((), ())),
                                    preferred_element_type=F32)
            GS[slot, :, pl.ds(pl.multiple_of(xh_ * 256, 256), 256)] = value.astype(BF16)

        each(0, 2, column)
        put(i, slot).start()
        gi_done.append(i)

    def open_up():
        pl.semaphore_wait(barrier, len(peers))
        w_copy.wait()
        for i in (0, 2, 1, 3):
            ag1(i).start()
        for copy in leaves[2:]:
            copy.start()
        for copy in cot_copies:
            copy.wait()

    def second_ag():
        ag1(0).wait_recv()
        for i in (2, 1, 3):
            ag1(i, 1).start()

    single = {"AG": open_up, "A2": second_ag, "F": finish}
    numbered = {"La": lambda s: leaf(s, 0), "Lb": lambda s: leaf(s, 1), "YA": y_forward, "XA": x_leaf, "YB": y_cross,
                "XB": x_forward, "C": close, "D": pass_on, "ha": own_hop, "hb": other_hop, "gi": grad_input}
    for event in EVENTS:
        if event in single:
            single[event]()
        else:
            numbered[event[:-1]](int(event[-1]))

    for i in gi_done[-2:]:
        put(i, gi_done.index(i) % 2).wait()
    for s in range(8):
        pltpu.make_async_copy(RB.at[s], RB.at[s], s_sem.at[s]).wait()
    for whose in range(2):
        for i in range(whose, 4):
            ag1(i, whose).wait_send()
    for i in range(8):
        for half in range(2):
            swap(i, half).wait_send()
    for i in (0,) + tuple(range(FAR, 9 - FAR)):
        across(i).wait_send()
    for k in range(1, 4):
        for way in range(2):
            ring(way, k, xh).wait_send()
            if k < FAR:
                ring(way, k, 1 - xh).wait_send()
    ring(c, 4, xh).wait_send()
    for s in range(7):
        g_copy(s).wait_send()
        for part in z_parts(s):
            z_copy(s, part).wait_send()
    for i in range(3):
        last_copy(i).wait_send()


def deliver(sums, products, grad_weight, grad_input, sem):
    copies = [pltpu.make_async_copy(products.at[pl.ds(i * 64, 64)], grad_input.at[pl.ds(i * 64, 64)], sem.at[i])
              for i in range(8)]
    for copy in copies:
        copy.start()
    for row in range(16):
        start = row % 2 * 1024
        grad_weight[row // 2:row // 2 + 1, start:start + 1024] = sums[row:row + 1, :]
    for copy in copies:
        copy.wait()


def local(unscale, inputs, cotangent, weight):
    dma = pltpu.SemaphoreType.DMA
    hbm = pl.BlockSpec(memory_space=pltpu.HBM)
    anywhere = pl.BlockSpec(memory_space=pl.ANY)
    vmem = pl.BlockSpec(memory_space=pltpu.VMEM)
    sums, products = pl.pallas_call(
        lambda *refs: kernel(unscale, *refs),
        out_shape=(jax.ShapeDtypeStruct((16, 1024), F32), jax.ShapeDtypeStruct((512, 4096), BF16)),
        in_specs=[hbm] * 3,
        out_specs=(vmem, anywhere),
        scratch_shapes=[
            pltpu.VMEM((512, 1024), BF16),
            pltpu.VMEM((8, 2, 512, 256), BF16),
            pltpu.VMEM((256, 1024), F32),
            pltpu.VMEM((8, 4, 4, 2, 16, 1024), BF16),
            pltpu.VMEM((8, 4, 7, 16, 1024), BF16),
            pltpu.VMEM((8, 2, 2, 4, 2, 16, 1024), BF16),
            pltpu.VMEM((64, 1024), F32),
            pltpu.VMEM((8, 2, 2, 16, 1024), BF16),
            pltpu.VMEM((7, 2, 16, 1024), BF16),
            pltpu.VMEM((7, 2, 16, 1024), BF16),
            pltpu.VMEM((3, 16, 1024), BF16),
            pltpu.VMEM((2, 512, 512), BF16),
            dma((11, 2)), dma((8,)), dma((8, 4, 4)),
            dma((8,)), dma((8,)), dma((8,)), dma((8,)), dma((16,)), dma((16,)), dma((16,)), dma((16,)),
            dma((7,)), dma((7,)), dma((14,)), dma((14,)), dma((3,)), dma((3,)), dma((2,)),
        ],
        compiler_params=pltpu.CompilerParams(collective_id=0, has_side_effects=True, vmem_limit_bytes=48 << 20),
        cost_estimate=pl.CostEstimate(flops=4 * 512 * 4096 * 1024, bytes_accessed=10 << 20, transcendentals=0),
        name="exchange",
    )(*[pltpu.with_memory_space_constraint(array, pltpu.HBM) for array in (inputs, cotangent, weight)])
    return pl.pallas_call(
        deliver,
        out_shape=(jax.ShapeDtypeStruct((8, 2048), F32), jax.ShapeDtypeStruct((512, 4096), BF16)),
        in_specs=[vmem, vmem],
        out_specs=(vmem, hbm),
        scratch_shapes=[dma((8,))],
        compiler_params=pltpu.CompilerParams(vmem_limit_bytes=16 << 20),
        name="deliver",
    )(sums, products)


def solution(mesh):
    sharded = P(("node", "local"), None)
    tokens = 512 * mesh.shape["node"] * mesh.shape["local"]
    unscale = 1.0 / math.sqrt(tokens)
    return jax.shard_map(lambda *args: local(unscale, *args), mesh=mesh, in_specs=(sharded,) * 3,
                         out_specs=(sharded,) * 2, check_vma=False)
```
